128 devices in a mesh: pf: 4 (over x), dp: 8 (over y, core), head: 4 (over z).
Axes of the slice: x: 4, y: 4, z: 4, core: 2. Of those that a mesh axis runs over, the one named last changes fastest.
Arguments:
- prompt_kv: bfloat16 [4, 32, 1024, 576], P('pf', ('dp', 'head')), may hold values from -6 to 6
- prompt_len: int32 [128], replicated, may hold values from 128 to 1024, as said below
- prefill_owner: int32 [128], replicated, may hold values from 0 to 3, as said below
- decode_list: int32 [32, 4], replicated, may hold values from 0 to 127, as said below
- positions: int32 [128], P(('pf', 'dp')), may hold values from 1024 to 2047
- query: bfloat16 [4, 128, 64, 192], P(None, ('pf', 'dp'), 'head'), may hold values from -70 to 70
- new_kv: bfloat16 [4, 128, 576], P(None, ('pf', 'dp')), may hold values from -6 to 6
- w_uk: bfloat16 [64, 128, 512], P('head'), may hold values from -0.5 to 0.5
- w_uv: bfloat16 [64, 512, 128], P('head'), may hold values from -0.25 to 0.25
- w_out: bfloat16 [8192, 7168], P('head', 'pf'), may hold values from -0.0625 to 0.0625
Outputs:
- out_rows: bfloat16 [4, 128, 7168], P(None, ('pf', 'dp'))
The draws below stay inside these ranges and needn't reach their ends.
Inputs may be any that keep to these rules, and one draw needn't show every extreme that they name: `prompt_len`: some request has exactly 1024 rows. `prefill_owner`: each row of decode_list holds exactly one request of each prefill group. `decode_list`: every request appears exactly once.
All inputs are finite; a program needn't handle non-finite values.
Results may differ from the reference program's by a relative error of at most 0.0075.
The reference program's roundings to bfloat16 on the way count: a program that leaves them out, or rounds other values in their place, can miss the bound.
Values may be sent and summed in bfloat16 or wider, within the bound.
No kernel may reach another device: no remote copies, remote signals or barrier semaphores. Data moves between devices by JAX's collectives and lax.ppermute only.
A program may use at most 64 MiB of HBM per device.

```python
import jax
import jax.numpy as jnp
from jax import lax

D = 7168
HEADS = 64
LATENT = 512
ROPE = 64
NOPE = 128
VDIM = 128
LMAX = 1024
STEPS = 4
SEQ_DEV = 4
DECODERS = 32
SEQS = 128
STRIPES = 32
CAP = 32
KVW = 576
N_PF = 4


def assignment(key):
    return jax.random.permutation(key, SEQS).astype(jnp.int32).reshape(DECODERS, SEQ_DEV)


def draw_prefill_owner(key, part):
    base_rows = assignment(key)
    groups = jnp.broadcast_to(jnp.arange(SEQ_DEV, dtype=jnp.int32)[None, :], (DECODERS, SEQ_DEV))
    return jnp.zeros((SEQS,), jnp.int32).at[base_rows.reshape(-1)].set(groups.reshape(-1))


def draw_decode_list(key, part):
    base_rows = assignment(key)
    key = jax.random.fold_in(key, 12)
    return jax.random.permutation(key, base_rows, axis=1, independent=True).astype(jnp.int32)


def draw_prompt_len(key, part):
    key = jax.random.fold_in(key, 13)
    first, second = jax.random.split(key)
    lengths = jax.random.randint(first, (SEQS,), LMAX // 8, LMAX + 1)
    longest = jax.random.randint(second, (), 0, SEQS)
    return lengths.at[longest].set(LMAX).astype(jnp.int32)


def draw_query(key, part):
    key = jax.random.fold_in(key, 14)
    first = jax.random.fold_in(key, 0)
    full_shape = (STEPS, SEQS, HEADS, NOPE + ROPE)
    values = jnp.clip(jax.random.normal(first, full_shape) * 1.5, -9.0, 9.0)
    return values.astype(jnp.float32).astype(jnp.bfloat16)


def touch_ends(drawn, rng, smallest, top_value):
    longest = drawn.shape.index(max(drawn.shape))
    spots = []
    for shift in (0, 1):
        where = [jax.random.randint(jax.random.fold_in(rng, axis), (), 0, length) for axis, length in enumerate(drawn.shape)]
        where[longest] = (where[longest] + shift) % drawn.shape[longest]
        spots.append(tuple(where))
    return drawn.at[spots[0]].set(smallest).at[spots[1]].set(top_value)


def level_of(key, extent, pieces, least, top_value):
    loudness, own = 1.0, jax.random.fold_in(key, 6)
    for axis_at, blocks in pieces:
        heights = jnp.exp(jax.random.uniform(jax.random.fold_in(own, axis_at), (blocks,), jnp.float32, least / len(pieces), top_value / len(pieces)))
        loudness = loudness * jnp.repeat(heights, extent[axis_at] // blocks).reshape([-1 if axis == axis_at else 1 for axis in range(len(extent))])
    return loudness


def normal_values(stream_key, extent, spread, bound, cuts=(), kind=jnp.bfloat16):
    loudness = level_of(stream_key, extent, cuts, -0.22, 0.18) if cuts else 1.0
    values = jax.random.normal(stream_key, extent, jnp.float32) * spread * loudness
    return jnp.minimum(jnp.maximum(values, -bound), bound).astype(kind)


def setup_inputs(seed: int = 0) -> dict:
    seeds = jax.random.split(jax.random.key(seed), 11)
    prompt_kv = normal_values(seeds[0], (N_PF, STRIPES, DECODERS * CAP, KVW), 1.0, 6.0, ((0, 4), (1, 32)))
    prompt_len = draw_prompt_len(jax.random.fold_in(seeds[10], 71), 0)
    prefill_owner = draw_prefill_owner(jax.random.fold_in(seeds[10], 71), 0)
    decode_list = draw_decode_list(jax.random.fold_in(seeds[10], 71), 0)
    positions = touch_ends(jax.random.randint(seeds[4], (SEQS,), LMAX, 2 * LMAX), jax.random.fold_in(seeds[4], 1), LMAX, (2 * LMAX) - 1).astype(jnp.int32)
    query = draw_query(jax.random.fold_in(seeds[10], 71), 0)
    new_kv = normal_values(seeds[6], (STEPS, SEQS, KVW), 1.0, 6.0, ((1, 32),))
    w_uk = normal_values(seeds[7], (HEADS, NOPE, LATENT), NOPE ** -0.5, 0.5, ((0, 4),))
    w_uv = normal_values(seeds[8], (HEADS, LATENT, VDIM), LATENT ** -0.5, 0.25, ((0, 4),))
    w_out = normal_values(seeds[9], (HEADS * VDIM, D), (HEADS * VDIM) ** -0.5, 0.0625, ((0, 4), (1, 4)))
    return dict(prompt_kv=prompt_kv, prompt_len=prompt_len, prefill_owner=prefill_owner, decode_list=decode_list, positions=positions, query=query, new_kv=new_kv, w_uk=w_uk, w_uv=w_uv, w_out=w_out)


ROPE_BASE = 50000.0


def rotate(values, angle_pos):
    half_width = values.shape[-1] // 2
    frequency = ROPE_BASE ** (-(jnp.arange(half_width, dtype=jnp.float32) * 2.0 / values.shape[-1]))
    angles = angle_pos[..., None] * frequency
    cosine = jnp.cos(angles)
    sine_part = jnp.sin(angles)
    first = values[..., :half_width]
    second = values[..., half_width:]
    return jnp.concatenate([first * cosine - second * sine_part, second * cosine + first * sine_part], axis=-1)


def reference(prompt_kv, prompt_len, prefill_owner, decode_list, positions, query, new_kv, w_uk, w_uv, w_out):
    request_ids = jnp.arange(SEQS, dtype=jnp.int32)
    same_owner = prefill_owner[:, None] == prefill_owner[None, :]
    slot_rank = jnp.sum(same_owner & (request_ids[None, :] < request_ids[:, None]), axis=1).astype(jnp.int32)
    served = decode_list.reshape(-1)
    uk_wide = w_uk.astype(jnp.float32)
    uv_wide = w_uv.astype(jnp.float32)
    score_scale = (NOPE + ROPE) ** -0.5

    def serve_row(row_index):
        request = served[row_index]
        owning = prefill_owner[request]
        slot_index = slot_rank[request]
        prompt_rows = prompt_len[request]
        stripe_block = lax.dynamic_slice(prompt_kv, (owning.astype(jnp.int32), jnp.int32(0), (slot_index * CAP).astype(jnp.int32), jnp.int32(0)), (1, STRIPES, CAP, KVW))[0]
        cache_keys = stripe_block.transpose(1, 0, 2).reshape(LMAX, KVW)
        usable = jnp.arange(LMAX, dtype=jnp.int32) < prompt_rows
        query_rows = query[:, row_index].astype(jnp.float32)
        step_pos = (positions[row_index] + jnp.arange(STEPS, dtype=jnp.int32)).astype(jnp.float32)
        query_latent = jnp.einsum("shn,hnc->shc", query_rows[..., :NOPE], uk_wide).astype(jnp.bfloat16)
        query_rope = rotate(query_rows[..., NOPE:], step_pos[:, None]).astype(jnp.bfloat16)
        query_cat = jnp.concatenate([query_latent, query_rope], axis=-1).reshape(STEPS * HEADS, KVW).astype(jnp.float32)
        new_rows = new_kv[:, row_index]
        new_keys = jnp.concatenate([new_rows[:, :LATENT], rotate(new_rows[:, LATENT:].astype(jnp.float32), step_pos).astype(jnp.bfloat16)], axis=-1)
        keys_wide = cache_keys.astype(jnp.float32)
        new_wide = new_keys.astype(jnp.float32)
        cache_scores = jnp.dot(query_cat, keys_wide.T) * score_scale
        cache_scores = jnp.where(usable[None, :], cache_scores, -jnp.inf)
        new_scores = jnp.dot(query_cat, new_wide.T) * score_scale
        query_step = jnp.arange(STEPS * HEADS, dtype=jnp.int32) // HEADS
        causal = jnp.arange(STEPS, dtype=jnp.int32)[None, :] <= query_step[:, None]
        new_scores = jnp.where(causal, new_scores, -jnp.inf)
        row_max = jnp.maximum(jnp.max(cache_scores, axis=1), jnp.max(new_scores, axis=1))[:, None]
        cache_exp = jnp.exp(cache_scores - row_max)
        new_exp = jnp.exp(new_scores - row_max)
        row_total = jnp.sum(cache_exp, axis=1, keepdims=True) + jnp.sum(new_exp, axis=1, keepdims=True)
        cache_prob = (cache_exp / row_total).astype(jnp.bfloat16).astype(jnp.float32)
        new_prob = (new_exp / row_total).astype(jnp.bfloat16).astype(jnp.float32)
        latent_out = jnp.dot(cache_prob, keys_wide[:, :LATENT]) + jnp.dot(new_prob, new_wide[:, :LATENT])
        latent_out = latent_out.astype(jnp.bfloat16).reshape(STEPS, HEADS, LATENT).astype(jnp.float32)
        attended = jnp.einsum("shc,hcv->shv", latent_out, uv_wide).astype(jnp.bfloat16).reshape(STEPS, HEADS * VDIM)
        return jnp.dot(attended, w_out, preferred_element_type=jnp.float32).astype(jnp.bfloat16)

    out_rows = lax.map(serve_row, jnp.arange(SEQS, dtype=jnp.int32))
    return out_rows.transpose(1, 0, 2)
```

```python
import jax
import jax.numpy as jnp
from jax import lax
from jax.sharding import PartitionSpec as P

ROPE_BASE = 50000.0


def rotate(values, angle_pos):
    half_width = values.shape[-1] // 2
    frequency = ROPE_BASE ** (-(jnp.arange(half_width, dtype=jnp.float32) * 2.0 / values.shape[-1]))
    angles = angle_pos[..., None] * frequency
    cosine = jnp.cos(angles)
    sine_part = jnp.sin(angles)
    first = values[..., :half_width]
    second = values[..., half_width:]
    return jnp.concatenate(
        [first * cosine - second * sine_part, second * cosine + first * sine_part], axis=-1
    )


def pick(blocks, index):
    return lax.dynamic_index_in_dim(blocks, index, 0, keepdims=False)


def ring(value, axis, count, shift):
    if shift % count == 0:
        return value
    return lax.ppermute(value, axis, [(i, (i + shift) % count) for i in range(count)])


def plane(value, count, target):
    pairs = []
    for x in range(count):
        for z in range(count):
            to_x, to_z = target(x, z)
            pairs.append((x * count + z, (to_x % count) * count + to_z % count))
    return lax.ppermute(value, ("pf", "head"), pairs)


def shards(
    prompt_kv, prompt_len, prefill_owner, decode_list, positions, query, new_kv, w_uk, w_uv, w_out
):
    n = lax.axis_size("pf")
    dp_count = lax.axis_size("dp")
    stripes = dp_count * n
    decoders, seq_dev = decode_list.shape
    requests = decoders * seq_dev
    kv_width = prompt_kv.shape[3]
    capacity = prompt_kv.shape[2] // decoders
    step_count, _, head_dev, qk_width = query.shape
    nope_width = w_uk.shape[1]
    latent = w_uk.shape[2]
    my_x = lax.axis_index("pf")
    my_dp = lax.axis_index("dp")
    my_z = lax.axis_index("head")

    request_ids = jnp.arange(requests, dtype=jnp.int32)
    same_owner = prefill_owner[:, None] == prefill_owner[None, :]
    slot_rank = jnp.sum(same_owner & (request_ids[None, :] < request_ids[:, None]), axis=1)
    listed = decode_list[:, :, None] == request_ids[None, None, :]
    list_owner = jnp.sum(jnp.where(listed, prefill_owner[None, None, :], 0), axis=2)
    list_slot = jnp.sum(jnp.where(listed, slot_rank[None, None, :], 0), axis=2)
    list_len = jnp.sum(jnp.where(listed, prompt_len[None, None, :], 0), axis=2)
    from_here = list_owner == my_x
    send_slot = jnp.sum(jnp.where(from_here, list_slot, 0), axis=1)
    send_len = jnp.sum(jnp.where(from_here, list_len, 0), axis=1)
    local_slots = prompt_kv.reshape(decoders, capacity, kv_width)
    order = send_slot.reshape(n, dp_count).T.reshape(-1)
    outgoing = jnp.take(local_slots, order, axis=0)
    arrived = lax.all_to_all(outgoing, ("dp", "head"), split_axis=0, concat_axis=0, tiled=True)
    keys = arrived.reshape(stripes * capacity, kv_width)
    length = send_len[my_z * dp_count + my_dp]

    decoder = my_x * dp_count + my_dp
    my_owner = lax.dynamic_index_in_dim(list_owner, decoder, 0, keepdims=False)
    chosen = my_owner[None, :] == jnp.arange(n, dtype=jnp.int32)[:, None]
    chosen_seq = jnp.sum(
        jnp.where(chosen, jnp.arange(seq_dev, dtype=jnp.int32)[None, :], 0), axis=1
    )
    group_pos = jnp.sum(jnp.where(chosen, positions[None, :], 0), axis=1)
    query_chosen = jnp.take(query, chosen_seq, axis=1)
    new_chosen = jnp.take(new_kv, chosen_seq, axis=1)
    step_pos = (group_pos[None, :] + jnp.arange(step_count, dtype=jnp.int32)[:, None]).astype(
        jnp.float32
    )
    query_latent = jnp.einsum(
        "sphn,hnc->sphc", query_chosen[..., :nope_width], w_uk, preferred_element_type=jnp.float32
    ).astype(jnp.bfloat16)
    query_rope = rotate(
        query_chosen[..., nope_width:].astype(jnp.float32), step_pos[:, :, None]
    ).astype(jnp.bfloat16)
    query_cat = (
        jnp.concatenate([query_latent, query_rope], axis=-1)
        .transpose(1, 0, 2, 3)
        .reshape(n, step_count * head_dev, kv_width)
    )
    new_rope = rotate(new_chosen[..., latent:].astype(jnp.float32), step_pos).astype(jnp.bfloat16)
    new_keys = jnp.concatenate([new_chosen[..., :latent], new_rope], axis=-1).transpose(1, 0, 2)
    packed = jnp.concatenate([query_cat, new_keys], axis=1)
    rows = step_count * head_dev
    got = [
        plane(pick(packed, (my_z + k) % n), n, lambda x, z, k=k: (z + k, x)) for k in range(n)
    ]
    queries = jnp.concatenate([piece[:rows] for piece in got], axis=0)
    fresh = got[0][rows:]

    score_scale = qk_width ** (-0.5)
    cache_scores = (
        jnp.einsum("qc,kc->qk", queries, keys, preferred_element_type=jnp.float32) * score_scale
    )
    slot_ids = jnp.arange(stripes * capacity, dtype=jnp.int32)
    position = slot_ids % capacity * stripes + slot_ids // capacity
    cache_scores = jnp.where((position < length)[None, :], cache_scores, -jnp.inf)
    new_scores = (
        jnp.einsum("qc,kc->qk", queries, fresh, preferred_element_type=jnp.float32) * score_scale
    )
    query_step = jnp.arange(n * rows, dtype=jnp.int32) // head_dev % step_count
    causal = jnp.arange(step_count, dtype=jnp.int32)[None, :] <= query_step[:, None]
    new_scores = jnp.where(causal, new_scores, -jnp.inf)
    row_max = jnp.maximum(jnp.max(cache_scores, axis=1), jnp.max(new_scores, axis=1))[:, None]
    cache_exp = jnp.exp(cache_scores - row_max)
    new_exp = jnp.exp(new_scores - row_max)
    row_total = jnp.sum(cache_exp, axis=1, keepdims=True) + jnp.sum(new_exp, axis=1, keepdims=True)
    cache_prob = (cache_exp / row_total).astype(jnp.bfloat16)
    new_prob = (new_exp / row_total).astype(jnp.bfloat16)
    latent_full = jnp.einsum(
        "qk,kc->qc", cache_prob, keys[:, :latent], preferred_element_type=jnp.float32
    ) + jnp.einsum(
        "qk,kc->qc", new_prob, fresh[:, :latent], preferred_element_type=jnp.float32
    )
    latent_out = latent_full.astype(jnp.bfloat16).reshape(n, rows, latent)

    back = jnp.stack(
        [ring(pick(latent_out, (my_x - my_z - j) % n), "head", n, j) for j in range(n)]
    ).reshape(n, step_count, head_dev, latent)
    attended = jnp.einsum(
        "jshc,hcv->jshv", back, w_uv, preferred_element_type=jnp.float32
    ).astype(jnp.bfloat16)
    attended = attended.reshape(n * step_count, -1)
    gathered = jnp.stack([ring(attended, "pf", n, i) for i in range(n)])
    columns = w_out.shape[1]
    partial_value = jnp.einsum(
        "if,fd->id", gathered.reshape(n * n * step_count, -1), w_out,
        preferred_element_type=jnp.float32,
    ).astype(jnp.bfloat16).reshape(n, n, step_count, columns)
    summed = sum(
        ring(partial_value[:, j], "head", n, -j).astype(jnp.float32) for j in range(n)
    ).astype(jnp.bfloat16)
    final = jnp.stack([plane(summed, n, lambda x, z, k=k: (z, x + k)) for k in range(n)])
    x_ids = jnp.arange(n, dtype=jnp.int32)
    source = (my_z - x_ids)[None, :] % n * n + (x_ids[None, :] - my_owner[:, None]) % n
    out = jnp.take(final.reshape(n * n, step_count, columns), source, axis=0)
    return out.transpose(2, 0, 1, 3).reshape(step_count, seq_dev, n * columns)


def solution(mesh):
    placed = (
        P("pf", ("dp", "head"), None, None),
        P(),
        P(),
        P(),
        P(("pf", "dp")),
        P(None, ("pf", "dp"), "head", None),
        P(None, ("pf", "dp"), None),
        P("head", None, None),
        P("head", None, None),
        P("head", "pf"),
    )
    return jax.shard_map(
        shards, mesh=mesh, in_specs=placed, out_specs=P(None, ("pf", "dp"), None), check_vma=False
    )
```

```python
import jax
import jax.numpy as jnp
from jax import lax
from jax.experimental import pallas as pl
from jax.experimental.pallas import tpu as pltpu
from jax.sharding import PartitionSpec as P

ROPE_BASE = 50000.0


def rotate(values, angle_pos):
    half_width = values.shape[-1] // 2
    frequency = ROPE_BASE ** (-(jnp.arange(half_width, dtype=jnp.float32) * 2.0 / values.shape[-1]))
    angles = angle_pos[..., None] * frequency
    cosine = jnp.cos(angles)
    sine_part = jnp.sin(angles)
    first = values[..., :half_width]
    second = values[..., half_width:]
    return jnp.concatenate(
        [first * cosine - second * sine_part, second * cosine + first * sine_part], axis=-1
    )


def pick(blocks, index):
    return lax.dynamic_index_in_dim(blocks, index, 0, keepdims=False)


def ring(value, axis, count, shift):
    if shift % count == 0:
        return value
    return lax.ppermute(value, axis, [(i, (i + shift) % count) for i in range(count)])


def plane(value, count, target):
    pairs = []
    for x in range(count):
        for z in range(count):
            to_x, to_z = target(x, z)
            pairs.append((x * count + z, (to_x % count) * count + to_z % count))
    return lax.ppermute(value, ("pf", "head"), pairs)


SMEM = pl.BlockSpec(memory_space=pltpu.SMEM)
VMEM = pl.BlockSpec(memory_space=pltpu.VMEM)
LANES = 128
MIB = 1024 * 1024


def owned_by(list_ref, owner_ref, decoder, seq_dev, group):
    found = list_ref[decoder, 0]
    for n in range(1, seq_dev):
        request = list_ref[decoder, n]
        found = jnp.where(owner_ref[request] == group, request, found)
    return found


def pack_kernel(place_ref, owner_ref, list_ref, prompt_ref, out_ref, rank_ref):
    decoders, seq_dev = list_ref.shape
    capacity = prompt_ref.shape[0] // decoders
    tiles = prompt_ref.shape[1] // LANES
    half = capacity // 2
    my_x, dp_count, n = place_ref[0], place_ref[3], place_ref[4]
    count = jnp.int32(0)
    for request in range(decoders * seq_dev):
        rank_ref[request] = count
        count = count + jnp.where(owner_ref[request] == my_x, 1, 0)

    def move(decoder, _):
        slot = rank_ref[owned_by(list_ref, owner_ref, decoder, seq_dev, my_x)]
        target = decoder % dp_count * n + decoder // dp_count
        rows = pl.ds(pl.multiple_of(slot * capacity, capacity), capacity)
        for t in range(tiles):
            out_ref[target, t * capacity : (t + 1) * capacity, :] = prompt_ref[
                rows, t * LANES : (t + 1) * LANES
            ]
        rope = prompt_ref[rows, tiles * LANES :]
        out_ref[target, tiles * capacity :, :] = jnp.concatenate(
            [rope[:half], rope[half:]], axis=1
        )
        return 0

    lax.fori_loop(0, decoders, move, 0, unroll=4)


def attend_kernel(
    scale, steps, place_ref, owner_ref, list_ref, len_ref, kv_ref, *refs
):
    piece_refs, out_refs, query_ref = refs[:4], refs[4:8], refs[8]
    my_x, my_dp, my_z, dp_count, n = (place_ref[i] for i in range(5))
    stripes, packed_rows, _ = kv_ref.shape
    width = piece_refs[0].shape[1]
    rope_width = width % LANES
    tiles = width // LANES
    capacity = packed_rows * LANES // width
    half = capacity // 2
    block = out_refs[0].shape[0]
    heads = block // steps
    seq_dev = list_ref.shape[1]
    length = len_ref[owned_by(list_ref, owner_ref, my_z * dp_count + my_dp, seq_dev, my_x)]
    for k in range(4):
        at = lax.rem(my_x - my_z - k + 2 * n, n)
        query_ref[at, :, :] = piece_refs[k][:block, :]
    queries = query_ref[...].reshape(4 * block, width)
    plain = queries[:, : tiles * LANES]
    rope = queries[:, tiles * LANES :]
    blank = jnp.zeros_like(rope)
    fresh = piece_refs[0][block:, :]
    new_rows = fresh.shape[0]
    sides = [
        jnp.concatenate([plain, rope, blank], axis=1),
        jnp.concatenate([plain, blank, rope], axis=1),
    ]
    rope_keys = kv_ref[:, tiles * capacity :, :].reshape(stripes * half, LANES)
    scores, values = [], []
    for side in range(2):
        parts = [
            kv_ref[:, t * capacity + side * half : t * capacity + (side + 1) * half, :].reshape(
                stripes * half, LANES
            )
            for t in range(tiles)
        ]
        latents = jnp.concatenate(parts, axis=1)
        values.append(latents)
        keys = jnp.concatenate([latents, rope_keys], axis=1)
        score = lax.dot_general(
            sides[side], keys, (((1,), (1,)), ((), ())), preferred_element_type=jnp.float32
        ) * scale
        key_id = lax.broadcasted_iota(jnp.int32, (1, stripes * half), 1)
        position = (side * half + key_id % half) * stripes + key_id // half
        scores.append(jnp.where(position < length, score, -jnp.inf))
    score = lax.dot_general(
        queries, fresh, (((1,), (1,)), ((), ())), preferred_element_type=jnp.float32
    ) * scale
    step = lax.broadcasted_iota(jnp.int32, score.shape, 0) // heads % steps
    new_id = lax.broadcasted_iota(jnp.int32, score.shape, 1)
    scores.append(jnp.where(new_id <= step, score, -jnp.inf))
    values.append(fresh[:, : tiles * LANES])
    peak = jnp.maximum(
        jnp.max(jnp.maximum(scores[0], scores[1]), axis=1, keepdims=True),
        jnp.max(scores[2], axis=1, keepdims=True),
    )
    weights = [jnp.exp(score - peak) for score in scores]
    total = jnp.sum(weights[0] + weights[1], axis=1, keepdims=True) + jnp.sum(
        weights[2], axis=1, keepdims=True
    )
    share = 1.0 / total
    mixed = sum(
        jnp.dot((weight * share).astype(jnp.bfloat16), value, preferred_element_type=jnp.float32)
        for weight, value in zip(weights, values)
    ).astype(jnp.bfloat16)
    for j in range(4):
        out_refs[j][...] = mixed[j * block : (j + 1) * block, :]


def final_kernel(place_ref, owner_ref, list_ref, *refs):
    piece_refs, out_ref = refs[:4], refs[4]
    my_x, my_dp, my_z, dp_count, n = (place_ref[i] for i in range(5))
    steps, seq_dev, _ = out_ref.shape
    columns = piece_refs[0].shape[1]
    decoder = my_x * dp_count + my_dp
    shape = (steps * seq_dev, 4 * steps)
    row = lax.broadcasted_iota(jnp.int32, shape, 0)
    source = lax.broadcasted_iota(jnp.int32, shape, 1)
    for k in range(4):
        x = lax.rem(my_z - k + n, n)
        wanted = jnp.zeros(shape, jnp.int32)
        for seq in range(seq_dev):
            owner = owner_ref[list_ref[decoder, seq]]
            wanted = jnp.where(row % seq_dev == seq, lax.rem(x - owner + n, n), wanted)
        choose = (source // steps == wanted) & (source % steps == row // seq_dev)
        chosen = jnp.dot(
            jnp.where(choose, 1.0, 0.0).astype(jnp.bfloat16),
            piece_refs[k][...],
            preferred_element_type=jnp.float32,
        ).astype(jnp.bfloat16)
        at = pl.ds(pl.multiple_of(x * columns, LANES), columns)
        for s in range(steps):
            out_ref[s, :, at] = chosen[s * seq_dev : (s + 1) * seq_dev, :]


def shards(
    prompt_kv, prompt_len, prefill_owner, decode_list, positions, query, new_kv, w_uk, w_uv, w_out
):
    n = lax.axis_size("pf")
    dp_count = lax.axis_size("dp")
    stripes = dp_count * n
    decoders, seq_dev = decode_list.shape
    requests = decoders * seq_dev
    kv_width = prompt_kv.shape[3]
    capacity = prompt_kv.shape[2] // decoders
    step_count, _, head_dev, qk_width = query.shape
    nope_width = w_uk.shape[1]
    latent = w_uk.shape[2]
    my_x = lax.axis_index("pf")
    my_dp = lax.axis_index("dp")
    my_z = lax.axis_index("head")
    place = jnp.stack(
        [my_x, my_dp, my_z, jnp.int32(dp_count), jnp.int32(n)] + [jnp.int32(0)] * 3
    ).astype(jnp.int32)

    packed_rows = capacity * kv_width // LANES
    outgoing = pl.pallas_call(
        pack_kernel,
        out_shape=jax.ShapeDtypeStruct((stripes, packed_rows, LANES), prompt_kv.dtype),
        in_specs=[SMEM, SMEM, SMEM, VMEM],
        out_specs=VMEM,
        scratch_shapes=[pltpu.SMEM((requests,), jnp.int32)],
        compiler_params=pltpu.CompilerParams(vmem_limit_bytes=8 * MIB),
        name="pack_rows",
    )(place, prefill_owner, decode_list, prompt_kv.reshape(decoders * capacity, kv_width))
    arrived = lax.all_to_all(outgoing, ("dp", "head"), split_axis=0, concat_axis=0, tiled=True)

    decoder = my_x * dp_count + my_dp
    mine = lax.dynamic_index_in_dim(decode_list, decoder, 0, keepdims=False)
    hit = mine[:, None] == jnp.arange(requests, dtype=jnp.int32)[None, :]
    my_owner = jnp.sum(jnp.where(hit, prefill_owner[None, :], 0), axis=1)
    step_pos = (positions[None, :] + jnp.arange(step_count, dtype=jnp.int32)[:, None]).astype(
        jnp.float32
    )
    query_latent = jnp.einsum(
        "snhd,hdc->snhc", query[..., :nope_width], w_uk, preferred_element_type=jnp.float32
    ).astype(jnp.bfloat16)
    query_rope = rotate(query[..., nope_width:].astype(jnp.float32), step_pos[:, :, None]).astype(
        jnp.bfloat16
    )
    rows = step_count * head_dev
    query_cat = (
        jnp.concatenate([query_latent, query_rope], axis=-1)
        .transpose(1, 0, 2, 3)
        .reshape(seq_dev, rows, kv_width)
    )
    new_rope = rotate(new_kv[..., latent:].astype(jnp.float32), step_pos).astype(jnp.bfloat16)
    new_keys = jnp.concatenate([new_kv[..., :latent], new_rope], axis=-1).transpose(1, 0, 2)
    new_keys = jnp.pad(new_keys, ((0, 0), (0, 16 - step_count), (0, 0)))
    packed = jnp.concatenate([query_cat, new_keys], axis=1)
    got = []
    for k in range(n):
        seq = jnp.sum(
            jnp.where(my_owner == (my_z + k) % n, jnp.arange(seq_dev, dtype=jnp.int32), 0)
        )
        got.append(plane(pick(packed, seq), n, lambda x, z, k=k: (z + k, x)))

    latent_out = pl.pallas_call(
        lambda *refs: attend_kernel(qk_width ** (-0.5), step_count, *refs),
        out_shape=[jax.ShapeDtypeStruct((rows, latent), jnp.bfloat16)] * 4,
        in_specs=[SMEM, SMEM, SMEM, SMEM] + [VMEM] * 5,
        out_specs=[VMEM] * 4,
        scratch_shapes=[pltpu.VMEM((n, rows, kv_width), jnp.bfloat16)],
        compiler_params=pltpu.CompilerParams(vmem_limit_bytes=24 * MIB),
        name="attend",
    )(place, prefill_owner, decode_list, prompt_len, arrived, *got)

    back = jnp.stack([ring(latent_out[j], "head", n, j) for j in range(n)]).reshape(
        n, step_count, head_dev, latent
    )
    attended = jnp.einsum(
        "jshc,hcv->jshv", back, w_uv, preferred_element_type=jnp.float32
    ).astype(jnp.bfloat16)
    attended = attended.reshape(n * step_count, -1)
    gathered = jnp.stack([ring(attended, "pf", n, i) for i in range(n)])
    columns = w_out.shape[1]
    partial_value = jnp.einsum(
        "if,fd->id", gathered.reshape(n * n * step_count, -1), w_out,
        preferred_element_type=jnp.float32,
    ).astype(jnp.bfloat16).reshape(n, n, step_count, columns)
    summed = sum(
        ring(partial_value[:, j], "head", n, -j).astype(jnp.float32) for j in range(n)
    ).astype(jnp.bfloat16).reshape(n * step_count, columns)
    final = [plane(summed, n, lambda x, z, k=k: (z, x + k)) for k in range(n)]
    return pl.pallas_call(
        final_kernel,
        out_shape=jax.ShapeDtypeStruct((step_count, seq_dev, n * columns), jnp.bfloat16),
        in_specs=[SMEM, SMEM, SMEM] + [VMEM] * 4,
        out_specs=VMEM,
        compiler_params=pltpu.CompilerParams(vmem_limit_bytes=8 * MIB),
        name="assemble",
    )(place, prefill_owner, decode_list, *final)


def solution(mesh):
    placed = (
        P("pf", ("dp", "head"), None, None),
        P(),
        P(),
        P(),
        P(("pf", "dp")),
        P(None, ("pf", "dp"), "head", None),
        P(None, ("pf", "dp"), None),
        P("head", None, None),
        P("head", None, None),
        P("head", "pf"),
    )
    return jax.shard_map(
        shards, mesh=mesh, in_specs=placed, out_specs=P(None, ("pf", "dp"), None), check_vma=False
    )
```

```python
import jax
import jax.numpy as jnp
from jax import lax
from jax.experimental import pallas as pl
from jax.experimental.pallas import tpu as pltpu
from jax.sharding import PartitionSpec as P

ROPE_BASE = 50000.0


def ring(value, axis, count, shift):
    if shift % count == 0:
        return value
    return lax.ppermute(value, axis, [(i, (i + shift) % count) for i in range(count)])


def plane(value, count, target):
    pairs = []
    for x in range(count):
        for z in range(count):
            to_x, to_z = target(x, z)
            pairs.append((x * count + z, (to_x % count) * count + to_z % count))
    return lax.ppermute(value, ("pf", "head"), pairs)


SMEM = pl.BlockSpec(memory_space=pltpu.SMEM)
VMEM = pl.BlockSpec(memory_space=pltpu.VMEM)
ANY = pl.BlockSpec(memory_space=pl.ANY)
LANES = 128
MIB = 1024 * 1024


def owned_by(list_ref, owner_ref, decoder, group):
    found = list_ref[0, decoder]
    for n in range(1, list_ref.shape[0]):
        request = list_ref[n, decoder]
        found = jnp.where(owner_ref[request] == group, request, found)
    return found


def pack_kernel(place_ref, owner_ref, list_ref, prompt_ref, out_ref, rank_ref, flat_ref,
                rows_ref, block_ref, in_sems, out_sem):
    seq_dev, decoders = list_ref.shape
    width, total = flat_ref.shape
    capacity = total // decoders
    tiles = width // LANES
    half = capacity // 2
    chunks = in_sems.shape[0]
    span = total // chunks
    my_x, dp_count, n = place_ref[0], place_ref[3], place_ref[4]
    loads = []
    for c in range(chunks):
        at = slice(c * span, (c + 1) * span)
        load = pltpu.make_async_copy(prompt_ref.at[:, at], flat_ref.at[:, at], in_sems.at[c])
        load.start()
        loads.append(load)
    count = jnp.int32(0)
    for request in range(decoders * seq_dev):
        rank_ref[request] = count
        count = count + jnp.where(owner_ref[request] == my_x, 1, 0)
    for c in range(chunks):
        loads[c].wait()
        at = slice(c * span, (c + 1) * span)
        rows_ref[at, :] = flat_ref[:, at].T

    def move(decoder, _):
        slot = rank_ref[owned_by(list_ref, owner_ref, decoder, my_x)]
        target = decoder % dp_count * n + decoder // dp_count
        rows = pl.ds(pl.multiple_of(slot * capacity, capacity), capacity)
        for t in range(tiles):
            block_ref[target, t * capacity : (t + 1) * capacity, :] = rows_ref[
                rows, t * LANES : (t + 1) * LANES
            ]
        rope = rows_ref[rows, tiles * LANES :]
        block_ref[target, tiles * capacity :, :] = jnp.concatenate(
            [rope[:half], rope[half:]], axis=1
        )
        pltpu.make_async_copy(block_ref.at[target], out_ref.at[target], out_sem).start()
        return 0

    lax.fori_loop(0, decoders, move, 0, unroll=4)
    pltpu.make_async_copy(block_ref, out_ref, out_sem).wait()


def query_kernel(place_ref, owner_ref, list_ref, pos_ref, freq_ref, query_ref, new_ref, w_ref,
                 *refs):
    out_refs, full_ref, turn_ref = refs[:4], refs[4], refs[5]
    my_x, my_dp, my_z, dp_count, n = (place_ref[i] for i in range(5))
    steps, seq_dev, heads, qk = query_ref.shape
    nope, latent = w_ref.shape[1], w_ref.shape[2]
    rope = qk - nope
    part = rope // 2
    pairs = steps * seq_dev
    rows = pairs * heads
    shape = (pairs, part)
    pair = lax.broadcasted_iota(jnp.int32, shape, 0)
    pos = pair // seq_dev
    for seq in range(seq_dev):
        pos = pos + jnp.where(pair % seq_dev == seq, pos_ref[seq], 0)
    angles = pos.astype(jnp.float32) * freq_ref[...]
    cosine, sine = jnp.cos(angles), jnp.sin(angles)
    along = jnp.concatenate([cosine, cosine], axis=1)
    across = jnp.concatenate([-sine, sine], axis=1)
    turn_ref[:, :rope] = along
    turn_ref[:, rope:] = across
    queries = query_ref[...].reshape(rows, qk)
    plain = queries[:, :nope]
    head = lax.broadcasted_iota(jnp.int32, (rows, nope), 0) % heads
    spread = jnp.concatenate(
        [jnp.where(head == h, plain, jnp.zeros_like(plain)) for h in range(heads)], axis=1
    )
    full_ref[:, :latent] = jnp.dot(
        spread, w_ref[...].reshape(heads * nope, latent), preferred_element_type=jnp.float32
    ).astype(jnp.bfloat16)
    blank = jnp.zeros((heads, rope), jnp.bfloat16)
    for p in range(pairs):
        value = queries[p * heads : (p + 1) * heads, nope:].astype(jnp.float32)
        other = jnp.concatenate([value[:, part:], value[:, :part]], axis=1)
        turned = value * turn_ref[p : p + 1, :rope] + other * turn_ref[p : p + 1, rope:]
        full_ref[p * heads : (p + 1) * heads, latent:] = jnp.concatenate(
            [turned.astype(jnp.bfloat16), blank], axis=1
        )
    fresh = jnp.concatenate([new_ref[s].astype(jnp.float32) for s in range(steps)], axis=0)
    value = fresh[:, latent:]
    other = jnp.concatenate([value[:, part:], value[:, :part]], axis=1)
    turned = value * along + other * across
    fresh = jnp.concatenate(
        [fresh[:, :latent], turned, jnp.zeros_like(turned)], axis=1
    ).astype(jnp.bfloat16)
    row = lax.broadcasted_iota(jnp.int32, (16, pairs), 0)
    source = lax.broadcasted_iota(jnp.int32, (16, pairs), 1)
    decoder = my_x * dp_count + my_dp
    for k in range(4):
        group = lax.rem(my_z + k, n)
        seq = jnp.int32(0)
        for m in range(1, seq_dev):
            seq = jnp.where(owner_ref[list_ref[m, decoder]] == group, m, seq)
        for s in range(steps):
            at = pl.ds(pl.multiple_of((s * seq_dev + seq) * heads, heads), heads)
            out_refs[k][s * heads : (s + 1) * heads, :] = full_ref[at, :]
        choose = (source // seq_dev == row) & (source % seq_dev == seq)
        out_refs[k][steps * heads :, :] = jnp.dot(
            jnp.where(choose, 1.0, 0.0).astype(jnp.bfloat16),
            fresh,
            preferred_element_type=jnp.float32,
        ).astype(jnp.bfloat16)


def attend_kernel(
    scale, steps, place_ref, owner_ref, list_ref, len_ref, kv_ref, *refs
):
    piece_refs, out_refs, query_ref = refs[:4], refs[4:8], refs[8]
    my_x, my_dp, my_z, dp_count, n = (place_ref[i] for i in range(5))
    stripes, packed_rows, _ = kv_ref.shape
    block, latent = out_refs[0].shape
    width = piece_refs[0].shape[1]
    tiles = latent // LANES
    half = packed_rows - 2 * tiles * (packed_rows // (2 * tiles + 1))
    capacity = 2 * half
    heads = block // steps
    length = len_ref[owned_by(list_ref, owner_ref, my_z * dp_count + my_dp, my_x)]
    for k in range(4):
        at = lax.rem(my_x - my_z - k + 2 * n, n)
        query_ref[at, :, :] = piece_refs[k][:block, :]
    queries = query_ref[...].reshape(4 * block, width)
    plain = queries[:, :latent]
    rope = queries[:, latent:]
    moved = jnp.concatenate([rope[:, LANES // 2 :], rope[:, : LANES // 2]], axis=1)
    sides = [queries, jnp.concatenate([plain, moved], axis=1)]
    fresh = piece_refs[0][block:, :]
    rope_keys = kv_ref[:, tiles * capacity :, :].reshape(stripes * half, LANES)
    scores, values = [], []
    for side in range(2):
        parts = [
            kv_ref[:, t * capacity + side * half : t * capacity + (side + 1) * half, :].reshape(
                stripes * half, LANES
            )
            for t in range(tiles)
        ]
        latents = jnp.concatenate(parts, axis=1)
        values.append(latents)
        keys = jnp.concatenate([latents, rope_keys], axis=1)
        score = lax.dot_general(
            sides[side], keys, (((1,), (1,)), ((), ())), preferred_element_type=jnp.float32
        ) * scale
        key_id = lax.broadcasted_iota(jnp.int32, (1, stripes * half), 1)
        position = (side * half + key_id % half) * stripes + key_id // half
        scores.append(jnp.where(position < length, score, -jnp.inf))
    score = lax.dot_general(
        queries, fresh, (((1,), (1,)), ((), ())), preferred_element_type=jnp.float32
    ) * scale
    step = lax.broadcasted_iota(jnp.int32, score.shape, 0) // heads % steps
    new_id = lax.broadcasted_iota(jnp.int32, score.shape, 1)
    scores.append(jnp.where(new_id <= step, score, -jnp.inf))
    values.append(fresh[:, :latent])
    peak = jnp.maximum(
        jnp.max(jnp.maximum(scores[0], scores[1]), axis=1, keepdims=True),
        jnp.max(scores[2], axis=1, keepdims=True),
    )
    weights = [jnp.exp(score - peak) for score in scores]
    total = jnp.sum(weights[0] + weights[1], axis=1, keepdims=True) + jnp.sum(
        weights[2], axis=1, keepdims=True
    )
    share = 1.0 / total
    mixed = sum(
        jnp.dot((weight * share).astype(jnp.bfloat16), value, preferred_element_type=jnp.float32)
        for weight, value in zip(weights, values)
    ).astype(jnp.bfloat16)
    for j in range(4):
        out_refs[j][...] = mixed[j * block : (j + 1) * block, :]


def project_kernel(place_ref, w_ref, *refs):
    piece_refs, out_ref, block_ref, sem = refs[:4], refs[4], refs[5], refs[6]
    my_x, my_z, n = place_ref[0], place_ref[2], place_ref[4]
    per = piece_refs[0].shape[0]
    steps = per // 4
    total = 4 * per
    row = lax.broadcasted_iota(jnp.int32, (total, total), 0)
    source = lax.broadcasted_iota(jnp.int32, (total, total), 1)
    from_x = (my_x - row // steps % 4 + n) % n
    from_z = (my_z - row // per + n) % n
    choose = source == (from_x * 4 + from_z) * steps + row % steps
    gathered = jnp.concatenate([piece[...] for piece in piece_refs], axis=0)
    ordered = jnp.dot(
        jnp.where(choose, 1.0, 0.0).astype(jnp.bfloat16),
        gathered,
        preferred_element_type=jnp.float32,
    ).astype(jnp.bfloat16)
    columns = w_ref.shape[1]
    span = 256
    for c in range(columns // span):
        at = slice(c * span, (c + 1) * span)
        block_ref[:, at] = jnp.dot(
            ordered, w_ref[:, at], preferred_element_type=jnp.float32
        ).astype(jnp.bfloat16)
    copies = [
        pltpu.make_async_copy(
            block_ref.at[w * per : (w + 1) * per], out_ref.at[w * 4 + z], sem.at[w * 4 + z]
        )
        for w in range(4)
        for z in range(4)
    ]
    for copy in copies:
        copy.start()
    for copy in copies:
        copy.wait()


def final_kernel(place_ref, owner_ref, list_ref, piece_ref, out_ref):
    my_x, my_dp, dp_count = place_ref[0], place_ref[1], place_ref[3]
    steps, seq_dev, _ = out_ref.shape
    columns = piece_ref.shape[2]
    decoder = my_x * dp_count + my_dp
    shape = (steps * seq_dev, 4 * steps)
    row = lax.broadcasted_iota(jnp.int32, shape, 0)
    source = lax.broadcasted_iota(jnp.int32, shape, 1)
    wanted = jnp.zeros(shape, jnp.int32)
    for seq in range(seq_dev):
        owner = owner_ref[list_ref[seq, decoder]]
        wanted = jnp.where(row % seq_dev == seq, owner, wanted)
    choose = (source // steps == wanted) & (source % steps == row // seq_dev)
    choose = jnp.where(choose, 1.0, 0.0).astype(jnp.bfloat16)
    for x in range(4):
        summed = sum(piece_ref[x * 4 + h].astype(jnp.float32) for h in range(4))
        chosen = jnp.dot(
            choose, summed.astype(jnp.bfloat16), preferred_element_type=jnp.float32
        ).astype(jnp.bfloat16)
        for s in range(steps):
            out_ref[s, :, x * columns : (x + 1) * columns] = chosen[
                s * seq_dev : (s + 1) * seq_dev, :
            ]


def shards(
    prompt_kv, prompt_len, prefill_owner, decode_list, positions, query, new_kv, w_uk, w_uv, w_out
):
    n = lax.axis_size("pf")
    dp_count = lax.axis_size("dp")
    stripes = dp_count * n
    decoders, seq_dev = decode_list.shape
    requests = decoders * seq_dev
    kv_width = prompt_kv.shape[3]
    total = prompt_kv.shape[2]
    capacity = total // decoders
    step_count, _, head_dev, qk_width = query.shape
    latent = w_uk.shape[2]
    rope_width = kv_width - latent
    my_x = lax.axis_index("pf")
    my_dp = lax.axis_index("dp")
    my_z = lax.axis_index("head")
    place = jnp.stack(
        [my_x, my_dp, my_z, jnp.int32(dp_count), jnp.int32(n)] + [jnp.int32(0)] * 3
    ).astype(jnp.int32)
    served = decode_list.T

    packed_rows = capacity * kv_width // LANES
    outgoing = pl.pallas_call(
        pack_kernel,
        out_shape=jax.ShapeDtypeStruct((stripes, packed_rows, LANES), prompt_kv.dtype),
        in_specs=[SMEM, SMEM, SMEM, ANY],
        out_specs=ANY,
        scratch_shapes=[
            pltpu.SMEM((requests,), jnp.int32),
            pltpu.VMEM((kv_width, total), jnp.bfloat16),
            pltpu.VMEM((total, kv_width), jnp.bfloat16),
            pltpu.VMEM((stripes, packed_rows, LANES), jnp.bfloat16),
            pltpu.SemaphoreType.DMA((4,)),
            pltpu.SemaphoreType.DMA,
        ],
        compiler_params=pltpu.CompilerParams(vmem_limit_bytes=8 * MIB),
        name="pack_rows",
    )(place, prefill_owner, served, prompt_kv[0, 0].T)
    arrived = lax.all_to_all(outgoing, ("dp", "head"), split_axis=0, concat_axis=0, tiled=True)

    frequency = ROPE_BASE ** (
        -(jnp.arange(rope_width // 2, dtype=jnp.float32) * 2.0 / rope_width)
    )
    rows = step_count * head_dev
    wide = latent + LANES
    pieces = pl.pallas_call(
        query_kernel,
        out_shape=[jax.ShapeDtypeStruct((rows + 16, wide), jnp.bfloat16)] * 4,
        in_specs=[SMEM, SMEM, SMEM, SMEM] + [VMEM] * 4,
        out_specs=[VMEM] * 4,
        scratch_shapes=[
            pltpu.VMEM((seq_dev * rows, wide), jnp.bfloat16),
            pltpu.VMEM((step_count * seq_dev, 2 * rope_width), jnp.float32),
        ],
        compiler_params=pltpu.CompilerParams(vmem_limit_bytes=8 * MIB),
        name="project_queries",
    )(place, prefill_owner, served, positions, frequency[None, :], query, new_kv, w_uk)
    got = [plane(pieces[k], n, lambda x, z, k=k: (z + k, x)) for k in range(n)]

    latent_out = pl.pallas_call(
        lambda *refs: attend_kernel(qk_width ** (-0.5), step_count, *refs),
        out_shape=[jax.ShapeDtypeStruct((rows, latent), jnp.bfloat16)] * 4,
        in_specs=[SMEM, SMEM, SMEM, SMEM] + [VMEM] * 5,
        out_specs=[VMEM] * 4,
        scratch_shapes=[pltpu.VMEM((n, rows, wide), jnp.bfloat16)],
        compiler_params=pltpu.CompilerParams(vmem_limit_bytes=12 * MIB),
        name="attend",
    )(place, prefill_owner, served, prompt_len, arrived, *got)

    back = jnp.stack([ring(latent_out[j], "head", n, j) for j in range(n)]).reshape(
        n, step_count, head_dev, latent
    )
    attended = jnp.einsum(
        "jshc,hcv->jshv", back, w_uv, preferred_element_type=jnp.float32
    ).astype(jnp.bfloat16)
    attended = attended.reshape(n * step_count, -1)
    gathered = [ring(attended, "pf", n, i) for i in range(n)]
    columns = w_out.shape[1]
    partial_value = pl.pallas_call(
        project_kernel,
        out_shape=jax.ShapeDtypeStruct((n * n, n * step_count, columns), jnp.bfloat16),
        in_specs=[SMEM, VMEM] + [VMEM] * 4,
        out_specs=ANY,
        scratch_shapes=[
            pltpu.VMEM((n * n * step_count, columns), jnp.bfloat16),
            pltpu.SemaphoreType.DMA((n * n,)),
        ],
        compiler_params=pltpu.CompilerParams(vmem_limit_bytes=12 * MIB),
        name="project_out",
    )(place, w_out, *gathered)
    final = lax.all_to_all(
        partial_value, ("pf", "head"), split_axis=0, concat_axis=0, tiled=True
    )
    return pl.pallas_call(
        final_kernel,
        out_shape=jax.ShapeDtypeStruct((step_count, seq_dev, n * columns), jnp.bfloat16),
        in_specs=[SMEM, SMEM, SMEM, VMEM],
        out_specs=VMEM,
        compiler_params=pltpu.CompilerParams(vmem_limit_bytes=8 * MIB),
        name="assemble",
    )(place, prefill_owner, served, final)


def solution(mesh):
    placed = (
        P("pf", ("dp", "head"), None, None),
        P(),
        P(),
        P(),
        P(("pf", "dp")),
        P(None, ("pf", "dp"), "head", None),
        P(None, ("pf", "dp"), None),
        P("head", None, None),
        P("head", None, None),
        P("head", "pf"),
    )
    return jax.shard_map(
        shards, mesh=mesh, in_specs=placed, out_specs=P(None, ("pf", "dp"), None), check_vma=False
    )
```

```python
import functools

import jax
import jax.numpy as jnp
from jax import lax
from jax.experimental import pallas as pl
from jax.experimental.pallas import tpu as pltpu
from jax.sharding import PartitionSpec as P

ROPE_BASE = 50000.0


def ring(value, axis, count, shift):
    if shift % count == 0:
        return value
    return lax.ppermute(value, axis, [(i, (i + shift) % count) for i in range(count)])


def plane(value, count, target):
    pairs = []
    for x in range(count):
        for z in range(count):
            to_x, to_z = target(x, z)
            pairs.append((x * count + z, (to_x % count) * count + to_z % count))
    return lax.ppermute(value, ("pf", "head"), pairs)


SMEM = pl.BlockSpec(memory_space=pltpu.SMEM)
VMEM = pl.BlockSpec(memory_space=pltpu.VMEM)
HBM = pl.BlockSpec(memory_space=pltpu.HBM)
LANES = 128
MIB = 1024 * 1024
FULL = 125 * MIB // 2


def here():
    return lax.axis_index("pf"), lax.axis_index("dp"), lax.axis_index("head")


def owned_by(list_ref, owner_ref, decoder, group):
    found = list_ref[0, decoder]
    for n in range(1, list_ref.shape[0]):
        request = list_ref[n, decoder]
        found = jnp.where(owner_ref[request] == group, request, found)
    return found


def pack_kernel(dp_count, n, owner_hbm, list_hbm, prompt_ref, out_ref, owner_ref, list_ref,
                rank_ref, flat_ref, rows_ref, block_ref, small_sems, in_sems, out_sem):
    seq_dev, decoders = list_ref.shape
    width, total = flat_ref.shape
    capacity = total // decoders
    tiles = width // LANES
    half = capacity // 2
    chunks = in_sems.shape[0]
    span = total // chunks
    my_x, _, _ = here()
    scalars = [
        pltpu.make_async_copy(owner_hbm, owner_ref, small_sems.at[0]),
        pltpu.make_async_copy(list_hbm, list_ref, small_sems.at[1]),
    ]
    for load in scalars:
        load.start()
    loads = []
    for c in range(chunks):
        at = slice(c * span, (c + 1) * span)
        load = pltpu.make_async_copy(prompt_ref.at[:, at], flat_ref.at[:, at], in_sems.at[c])
        load.start()
        loads.append(load)
    for load in scalars:
        load.wait()
    count = jnp.int32(0)
    for request in range(decoders * seq_dev):
        rank_ref[request] = count
        count = count + jnp.where(owner_ref[request] == my_x, 1, 0)
    for c in range(chunks):
        loads[c].wait()
        at = slice(c * span, (c + 1) * span)
        rows_ref[at, :] = flat_ref[:, at].T

    def move(decoder, _):
        slot = rank_ref[owned_by(list_ref, owner_ref, decoder, my_x)]
        target = decoder % dp_count * n + decoder // dp_count
        rows = pl.ds(pl.multiple_of(slot * capacity, capacity), capacity)
        for t in range(tiles):
            block_ref[target, t * capacity : (t + 1) * capacity, :] = rows_ref[
                rows, t * LANES : (t + 1) * LANES
            ]
        rope = rows_ref[rows, tiles * LANES :]
        block_ref[target, tiles * capacity :, :] = jnp.concatenate(
            [rope[:half], rope[half:]], axis=1
        )
        pltpu.make_async_copy(block_ref.at[target], out_ref.at[target], out_sem).start()
        return 0

    lax.fori_loop(0, decoders, move, 0, unroll=4)
    pltpu.make_async_copy(block_ref, out_ref, out_sem).wait()


def query_kernel(dp_count, owner_ref, list_ref, pos_ref, freq_ref, query_hbm, new_hbm, w_hbm,
                 *refs):
    out_refs = refs[:4]
    full_ref, rope_ref, turn_ref, query_ref, new_ref, w_ref, sems = refs[4:]
    loads = [
        pltpu.make_async_copy(query_hbm, query_ref, sems.at[0]),
        pltpu.make_async_copy(new_hbm, new_ref, sems.at[1]),
        pltpu.make_async_copy(w_hbm, w_ref, sems.at[2]),
    ]
    for load in loads:
        load.start()
    my_x, my_dp, my_z = here()
    n = len(out_refs)
    steps, seq_dev, heads, qk = query_ref.shape
    nope, latent = w_ref.shape[1], w_ref.shape[2]
    rope = qk - nope
    part = rope // 2
    pairs = steps * seq_dev
    rows = pairs * heads
    shape = (pairs, part)
    pair = lax.broadcasted_iota(jnp.int32, shape, 0)
    pos = pair // seq_dev
    for seq in range(seq_dev):
        pos = pos + jnp.where(pair % seq_dev == seq, pos_ref[seq], 0)
    angles = pos.astype(jnp.float32) * freq_ref[...]
    cosine, sine = jnp.cos(angles), jnp.sin(angles)
    along = jnp.concatenate([cosine, cosine], axis=1)
    across = jnp.concatenate([-sine, sine], axis=1)
    turn_ref[:, :rope] = along
    turn_ref[:, rope:] = across
    loads[0].wait()
    queries = query_ref[...].reshape(rows, qk)
    plain = queries[:, :nope]
    head = lax.broadcasted_iota(jnp.int32, (rows, nope), 0) % heads
    spread = jnp.concatenate(
        [jnp.where(head == h, plain, jnp.zeros_like(plain)) for h in range(heads)], axis=1
    )
    for p in range(pairs):
        value = queries[p * heads : (p + 1) * heads, nope:].astype(jnp.float32)
        other = jnp.concatenate([value[:, part:], value[:, :part]], axis=1)
        turned = value * turn_ref[p : p + 1, :rope] + other * turn_ref[p : p + 1, rope:]
        turned = turned.astype(jnp.bfloat16)
        rope_ref[p * heads : (p + 1) * heads, :] = jnp.concatenate([turned, turned], axis=1)
    loads[1].wait()
    fresh = jnp.concatenate([new_ref[s].astype(jnp.float32) for s in range(steps)], axis=0)
    value = fresh[:, latent:]
    other = jnp.concatenate([value[:, part:], value[:, :part]], axis=1)
    turned = value * along + other * across
    fresh = jnp.concatenate(
        [fresh[:, :latent], turned, jnp.zeros_like(turned)], axis=1
    ).astype(jnp.bfloat16)
    loads[2].wait()
    full_ref[...] = jnp.dot(
        spread, w_ref[...].reshape(heads * nope, latent), preferred_element_type=jnp.float32
    ).astype(jnp.bfloat16)
    row = lax.broadcasted_iota(jnp.int32, (16, pairs), 0)
    source = lax.broadcasted_iota(jnp.int32, (16, pairs), 1)
    lane = lax.broadcasted_iota(jnp.int32, (heads, LANES), 1)
    decoder = my_x * dp_count + my_dp
    block = steps * heads
    tiles = latent // LANES
    packed = block * tiles
    for k in range(n):
        group = lax.rem(my_z + k, n)
        seq = jnp.int32(0)
        for m in range(1, seq_dev):
            seq = jnp.where(owner_ref[list_ref[m, decoder]] == group, m, seq)
        at = [
            pl.ds(pl.multiple_of((s * seq_dev + seq) * heads, heads), heads)
            for s in range(steps)
        ]
        for s in range(steps):
            for t in range(tiles):
                first = t * block + s * heads
                out_refs[k][first : first + heads, :] = full_ref[
                    at[s], t * LANES : (t + 1) * LANES
                ]
        for s in range(steps // 2):
            out_refs[k][packed + s * heads : packed + (s + 1) * heads, :] = jnp.where(
                lane < rope, rope_ref[at[s], :], rope_ref[at[s + steps // 2], :]
            )
        if k == 0:
            choose = (source // seq_dev == row) & (source % seq_dev == seq)
            chosen = jnp.dot(
                jnp.where(choose, 1.0, 0.0).astype(jnp.bfloat16),
                fresh,
                preferred_element_type=jnp.float32,
            ).astype(jnp.bfloat16)
            first = packed + block // 2
            for t in range(tiles + 1):
                out_refs[k][first + t * 16 : first + (t + 1) * 16, :] = chosen[
                    :, t * LANES : (t + 1) * LANES
                ]


def attend_kernel(
    scale, steps, dp_count, owner_ref, list_ref, len_ref, kv_ref, *refs
):
    n = 4
    piece_refs, out_refs, plain_ref, rope_refs = refs[:n], refs[n : 2 * n], refs[2 * n], refs[-2:]
    my_x, my_dp, my_z = here()
    stripes, packed_rows, _ = kv_ref.shape
    block, latent = out_refs[0].shape
    tiles = latent // LANES
    half = packed_rows - 2 * tiles * (packed_rows // (2 * tiles + 1))
    capacity = 2 * half
    heads = block // steps
    packed = tiles * block
    length = len_ref[owned_by(list_ref, owner_ref, my_z * dp_count + my_dp, my_x)]
    lane = lax.broadcasted_iota(jnp.int32, (block // 2, LANES), 1)
    low = lane < LANES // 2
    for k in range(n):
        at = lax.rem(my_x - my_z - k + 2 * n, n)
        for t in range(tiles):
            plain_ref[at, :, t * LANES : (t + 1) * LANES] = piece_refs[k][
                t * block : (t + 1) * block, :
            ]
        rope = piece_refs[k][packed : packed + block // 2, :]
        swapped = jnp.concatenate([rope[:, LANES // 2 :], rope[:, : LANES // 2]], axis=1)
        blank = jnp.zeros_like(rope)
        rope_refs[0][at, : block // 2, :] = jnp.where(low, rope, blank)
        rope_refs[0][at, block // 2 :, :] = jnp.where(low, swapped, blank)
        rope_refs[1][at, : block // 2, :] = jnp.where(low, blank, swapped)
        rope_refs[1][at, block // 2 :, :] = jnp.where(low, blank, rope)
    plain = plain_ref[...].reshape(n * block, latent)
    sides = [
        jnp.concatenate([plain, ref[...].reshape(n * block, LANES)], axis=1) for ref in rope_refs
    ]
    first = packed + block // 2
    fresh = jnp.concatenate(
        [piece_refs[0][first + t * 16 : first + (t + 1) * 16, :] for t in range(tiles + 1)], axis=1
    )
    rope_keys = kv_ref[:, tiles * capacity :, :].reshape(stripes * half, LANES)
    scores, values = [], []
    for side in range(2):
        parts = [
            kv_ref[:, t * capacity + side * half : t * capacity + (side + 1) * half, :].reshape(
                stripes * half, LANES
            )
            for t in range(tiles)
        ]
        latents = jnp.concatenate(parts, axis=1)
        values.append(latents)
        keys = jnp.concatenate([latents, rope_keys], axis=1)
        score = lax.dot_general(
            sides[side], keys, (((1,), (1,)), ((), ())), preferred_element_type=jnp.float32
        ) * scale
        key_id = lax.broadcasted_iota(jnp.int32, (1, stripes * half), 1)
        position = (side * half + key_id % half) * stripes + key_id // half
        scores.append(jnp.where(position < length, score, -jnp.inf))
    score = lax.dot_general(
        sides[0], fresh, (((1,), (1,)), ((), ())), preferred_element_type=jnp.float32
    ) * scale
    step = lax.broadcasted_iota(jnp.int32, score.shape, 0) // heads % steps
    new_id = lax.broadcasted_iota(jnp.int32, score.shape, 1)
    scores.append(jnp.where(new_id <= step, score, -jnp.inf))
    values.append(fresh[:, :latent])
    peak = jnp.maximum(
        jnp.max(jnp.maximum(scores[0], scores[1]), axis=1, keepdims=True),
        jnp.max(scores[2], axis=1, keepdims=True),
    )
    weights = [jnp.exp(score - peak) for score in scores]
    total = jnp.sum(weights[0] + weights[1], axis=1, keepdims=True) + jnp.sum(
        weights[2], axis=1, keepdims=True
    )
    share = 1.0 / total
    mixed = sum(
        jnp.dot((weight * share).astype(jnp.bfloat16), value, preferred_element_type=jnp.float32)
        for weight, value in zip(weights, values)
    ).astype(jnp.bfloat16)
    for j in range(n):
        out_refs[j][...] = mixed[j * block : (j + 1) * block, :]


def project_kernel(w_ref, *refs):
    n = 4
    piece_refs, out_ref, block_ref, sem = refs[:n], refs[n], refs[n + 1], refs[n + 2]
    my_x, _, my_z = here()
    per = piece_refs[0].shape[0]
    steps = per // n
    total = n * per
    columns = w_ref.shape[1]
    row = lax.broadcasted_iota(jnp.int32, (total, total), 0)
    source = lax.broadcasted_iota(jnp.int32, (total, total), 1)
    from_x = (my_x - row // steps % 4 + n) % n
    from_z = (my_z - row // per + n) % n
    choose = source == (from_x * 4 + from_z) * steps + row % steps
    gathered = jnp.concatenate([piece[...] for piece in piece_refs], axis=0)
    ordered = jnp.dot(
        jnp.where(choose, 1.0, 0.0).astype(jnp.bfloat16),
        gathered,
        preferred_element_type=jnp.float32,
    ).astype(jnp.bfloat16)
    copies = []
    span = 256
    chunks = columns // span
    groups = ((0, 4), (4, chunks))
    for g, (first, last) in enumerate(groups):
        for c in range(first, last):
            at = slice(c * span, (c + 1) * span)
            block_ref[:, at] = jnp.dot(
                ordered, w_ref[:, at], preferred_element_type=jnp.float32
            ).astype(jnp.bfloat16)
        at = slice(first * span, last * span)
        for w in range(4):
            for z in range(4):
                copy = pltpu.make_async_copy(
                    block_ref.at[w * per : (w + 1) * per, at],
                    out_ref.at[w * 4 + z, :, at],
                    sem.at[g, w * 4 + z],
                )
                copy.start()
                copies.append(copy)
    for copy in copies:
        copy.wait()


def load_kernel(after_ref, far_ref, near_ref, sem):
    load = pltpu.make_async_copy(far_ref, near_ref, sem)
    load.start()
    load.wait()


def bring_near(weight, after, room, name):
    return pl.pallas_call(
        load_kernel,
        out_shape=jax.ShapeDtypeStruct(weight.shape, weight.dtype),
        in_specs=[VMEM, HBM],
        out_specs=VMEM,
        scratch_shapes=[pltpu.SemaphoreType.DMA],
        compiler_params=pltpu.CompilerParams(vmem_limit_bytes=room * MIB),
        cost_estimate=pl.CostEstimate(
            flops=0, bytes_accessed=4 * weight.size, transcendentals=0
        ),
        name=name,
    )(after, weight)


def final_kernel(dp_count, owner_ref, list_ref, piece_ref, out_ref):
    my_x, my_dp, _ = here()
    steps, seq_dev, _ = out_ref.shape
    columns = piece_ref.shape[2]
    decoder = my_x * dp_count + my_dp
    shape = (steps * seq_dev, 4 * steps)
    row = lax.broadcasted_iota(jnp.int32, shape, 0)
    source = lax.broadcasted_iota(jnp.int32, shape, 1)
    wanted = jnp.zeros(shape, jnp.int32)
    for seq in range(seq_dev):
        owner = owner_ref[list_ref[seq, decoder]]
        wanted = jnp.where(row % seq_dev == seq, owner, wanted)
    choose = (source // steps == wanted) & (source % steps == row // seq_dev)
    choose = jnp.where(choose, 1.0, 0.0).astype(jnp.bfloat16)
    for x in range(4):
        summed = sum(piece_ref[x * 4 + h].astype(jnp.float32) for h in range(4))
        chosen = jnp.dot(
            choose, summed.astype(jnp.bfloat16), preferred_element_type=jnp.float32
        ).astype(jnp.bfloat16)
        for s in range(steps):
            out_ref[s, :, x * columns : (x + 1) * columns] = chosen[
                s * seq_dev : (s + 1) * seq_dev, :
            ]


def shards(
    prompt_kv, prompt_len, prefill_owner, decode_list, positions, query, new_kv, w_uk, w_uv, w_out
):
    n = lax.axis_size("pf")
    dp_count = lax.axis_size("dp")
    stripes = dp_count * n
    decoders, seq_dev = decode_list.shape
    requests = decoders * seq_dev
    kv_width = prompt_kv.shape[3]
    total = prompt_kv.shape[2]
    capacity = total // decoders
    step_count, _, head_dev, qk_width = query.shape
    latent = w_uk.shape[2]
    rope_width = kv_width - latent
    served = decode_list.T

    packed_rows = capacity * kv_width // LANES
    outgoing = pl.pallas_call(
        functools.partial(pack_kernel, dp_count, n),
        out_shape=jax.ShapeDtypeStruct((stripes, packed_rows, LANES), prompt_kv.dtype),
        in_specs=[HBM] * 3,
        out_specs=HBM,
        scratch_shapes=[
            pltpu.SMEM((requests,), jnp.int32),
            pltpu.SMEM((seq_dev, decoders), jnp.int32),
            pltpu.SMEM((requests,), jnp.int32),
            pltpu.VMEM((kv_width, total), jnp.bfloat16),
            pltpu.VMEM((total, kv_width), jnp.bfloat16),
            pltpu.VMEM((stripes, packed_rows, LANES), jnp.bfloat16),
            pltpu.SemaphoreType.DMA((2,)),
            pltpu.SemaphoreType.DMA((4,)),
            pltpu.SemaphoreType.DMA,
        ],
        compiler_params=pltpu.CompilerParams(vmem_limit_bytes=FULL),
        name="pack_rows",
    )(prefill_owner, served, prompt_kv[0, 0].T)
    arrived = lax.all_to_all(outgoing, ("dp", "head"), split_axis=0, concat_axis=0, tiled=True)

    frequency = ROPE_BASE ** (
        -(jnp.arange(rope_width // 2, dtype=jnp.float32) * 2.0 / rope_width)
    )
    rows = step_count * head_dev
    packed_query = rows * latent // LANES + rows // 2
    extra = 16 * (latent // LANES + 1)
    pieces = pl.pallas_call(
        functools.partial(query_kernel, dp_count),
        out_shape=[
            jax.ShapeDtypeStruct((packed_query + (extra if k == 0 else 0), LANES), jnp.bfloat16)
            for k in range(n)
        ],
        in_specs=[SMEM, SMEM, SMEM, VMEM] + [HBM] * 3,
        out_specs=[VMEM] * n,
        scratch_shapes=[
            pltpu.VMEM((seq_dev * rows, latent), jnp.bfloat16),
            pltpu.VMEM((seq_dev * rows, LANES), jnp.bfloat16),
            pltpu.VMEM((step_count * seq_dev, 2 * rope_width), jnp.float32),
            pltpu.VMEM(query.shape, query.dtype),
            pltpu.VMEM(new_kv.shape, new_kv.dtype),
            pltpu.VMEM(w_uk.shape, w_uk.dtype),
            pltpu.SemaphoreType.DMA((3,)),
        ],
        compiler_params=pltpu.CompilerParams(vmem_limit_bytes=FULL),
        name="project_queries",
    )(prefill_owner, served, positions, frequency[None, :], query, new_kv, w_uk)
    got = [plane(pieces[k], n, lambda x, z, k=k: (z + k, x)) for k in range(n)]

    latent_out = pl.pallas_call(
        functools.partial(attend_kernel, qk_width ** (-0.5), step_count, dp_count),
        out_shape=[jax.ShapeDtypeStruct((rows, latent), jnp.bfloat16)] * n,
        in_specs=[SMEM, SMEM, SMEM] + [VMEM] * (n + 1),
        out_specs=[VMEM] * n,
        scratch_shapes=[
            pltpu.VMEM((n, rows, latent), jnp.bfloat16),
            pltpu.VMEM((n, rows, LANES), jnp.bfloat16),
            pltpu.VMEM((n, rows, LANES), jnp.bfloat16),
        ],
        compiler_params=pltpu.CompilerParams(vmem_limit_bytes=12 * MIB),
        name="attend",
    )(prefill_owner, served, prompt_len, arrived, *got)
    w_uv = bring_near(w_uv, latent_out[0], 50, "load_w_uv")

    back = jnp.stack([ring(latent_out[j], "head", n, j) for j in range(n)]).reshape(
        n, step_count, head_dev, latent
    )
    attended = jnp.einsum(
        "jshc,hcv->jshv", back, w_uv, preferred_element_type=jnp.float32
    ).astype(jnp.bfloat16)
    attended = attended.reshape(n * step_count, -1)
    gathered = [ring(attended, "pf", n, i) for i in range(n)]
    w_out = bring_near(w_out, attended, 43, "load_w_out")
    columns = w_out.shape[1]
    partial_value = pl.pallas_call(
        project_kernel,
        out_shape=jax.ShapeDtypeStruct((n * n, n * step_count, columns), jnp.bfloat16),
        in_specs=[VMEM] * (n + 1),
        out_specs=HBM,
        scratch_shapes=[
            pltpu.VMEM((n * n * step_count, columns), jnp.bfloat16),
            pltpu.SemaphoreType.DMA((2, n * n)),
        ],
        compiler_params=pltpu.CompilerParams(vmem_limit_bytes=12 * MIB),
        name="project_out",
    )(w_out, *gathered)
    final = lax.all_to_all(
        partial_value, ("pf", "head"), split_axis=0, concat_axis=0, tiled=True
    )
    return pl.pallas_call(
        functools.partial(final_kernel, dp_count),
        out_shape=jax.ShapeDtypeStruct((step_count, seq_dev, n * columns), jnp.bfloat16),
        in_specs=[SMEM, SMEM, VMEM],
        out_specs=VMEM,
        compiler_params=pltpu.CompilerParams(vmem_limit_bytes=8 * MIB),
        name="assemble",
    )(prefill_owner, served, final)


def solution(mesh):
    placed = (
        P("pf", ("dp", "head"), None, None),
        P(),
        P(),
        P(),
        P(("pf", "dp")),
        P(None, ("pf", "dp"), "head", None),
        P(None, ("pf", "dp"), None),
        P("head", None, None),
        P("head", None, None),
        P("head", "pf"),
    )
    return jax.shard_map(
        shards, mesh=mesh, in_specs=placed, out_specs=P(None, ("pf", "dp"), None), check_vma=False
    )
```

```python
import functools

import jax
import jax.numpy as jnp
import numpy as np
from jax import lax
from jax.experimental import pallas as pl
from jax.experimental.pallas import tpu as pltpu
from jax.sharding import PartitionSpec as P

ROPE_BASE = 50000.0


def ring(value, axis, count, shift):
    if shift % count == 0:
        return value
    return lax.ppermute(value, axis, [(i, (i + shift) % count) for i in range(count)])


def plane(value, count, target):
    pairs = []
    for x in range(count):
        for z in range(count):
            to_x, to_z = target(x, z)
            pairs.append((x * count + z, (to_x % count) * count + to_z % count))
    return lax.ppermute(value, ("pf", "head"), pairs)


SMEM = pl.BlockSpec(memory_space=pltpu.SMEM)
VMEM = pl.BlockSpec(memory_space=pltpu.VMEM)
HBM = pl.BlockSpec(memory_space=pltpu.HBM)
LANES = 128
MIB = 1024 * 1024
FULL = 125 * MIB // 2


def here():
    return lax.axis_index("pf"), lax.axis_index("dp"), lax.axis_index("head")


def owned_by(list_ref, owner_ref, decoder, group):
    found = list_ref[0, decoder]
    for n in range(1, list_ref.shape[0]):
        request = list_ref[n, decoder]
        found = jnp.where(owner_ref[request] == group, request, found)
    return found


def pack_kernel(dp_count, n, owner_hbm, list_hbm, prompt_ref, out_ref, owner_ref, list_ref,
                rank_ref, target_ref, flat_ref, block_ref, small_sems, in_sems, out_sem):
    seq_dev, decoders = list_ref.shape
    width, total = flat_ref.shape
    capacity = total // decoders
    tiles = width // LANES
    half = capacity // 2
    chunks = in_sems.shape[0]
    span = total // chunks
    slots = decoders // chunks
    my_x, _, _ = here()
    scalars = [
        pltpu.make_async_copy(owner_hbm, owner_ref, small_sems.at[0]),
        pltpu.make_async_copy(list_hbm, list_ref, small_sems.at[1]),
    ]
    for load in scalars:
        load.start()
    loads = []
    for c in range(chunks):
        at = slice(c * span, (c + 1) * span)
        load = pltpu.make_async_copy(prompt_ref.at[:, at], flat_ref.at[:, at], in_sems.at[c])
        load.start()
        loads.append(load)
    for load in scalars:
        load.wait()
    count = jnp.int32(0)
    for request in range(decoders * seq_dev):
        rank_ref[request] = count
        count = count + jnp.where(owner_ref[request] == my_x, 1, 0)
    for decoder in range(decoders):
        slot = rank_ref[owned_by(list_ref, owner_ref, decoder, my_x)]
        target_ref[slot] = decoder % dp_count * n + decoder // dp_count
    for c in range(chunks):
        loads[c].wait()
        rows = flat_ref[:, c * span : (c + 1) * span].T
        for i in range(slots):
            slot = c * slots + i
            mine = rows[i * capacity : (i + 1) * capacity, :]
            for t in range(tiles):
                block_ref[slot, t * capacity : (t + 1) * capacity, :] = mine[
                    :, t * LANES : (t + 1) * LANES
                ]
            rope = mine[:, tiles * LANES :]
            block_ref[slot, tiles * capacity :, :] = jnp.concatenate(
                [rope[:half], rope[half:]], axis=1
            )
            pltpu.make_async_copy(
                block_ref.at[slot], out_ref.at[target_ref[slot]], out_sem
            ).start()
    pltpu.make_async_copy(block_ref, out_ref, out_sem).wait()


def query_kernel(dp_count, owner_ref, list_ref, len_ref, pos_ref, freq_ref, query_hbm, new_hbm,
                 w_hbm, *refs):
    out_refs, order_ref = refs[:4], refs[4]
    full_ref, rope_ref, turn_ref, query_ref, new_ref, w_ref, sems = refs[5:]
    loads = [
        pltpu.make_async_copy(query_hbm, query_ref, sems.at[0]),
        pltpu.make_async_copy(new_hbm, new_ref, sems.at[1]),
        pltpu.make_async_copy(w_hbm, w_ref, sems.at[2]),
    ]
    for load in loads:
        load.start()
    my_x, my_dp, my_z = here()
    n = len(out_refs)
    steps, seq_dev, heads, qk = query_ref.shape
    nope, latent = w_ref.shape[1], w_ref.shape[2]
    rope = qk - nope
    part = rope // 2
    pairs = steps * seq_dev
    rows = pairs * heads
    shape = (pairs, part)
    pair = lax.broadcasted_iota(jnp.int32, shape, 0)
    pos = pair // seq_dev
    for seq in range(seq_dev):
        pos = pos + jnp.where(pair % seq_dev == seq, pos_ref[seq], 0)
    angles = pos.astype(jnp.float32) * freq_ref[...]
    cosine, sine = jnp.cos(angles), jnp.sin(angles)
    along = jnp.concatenate([cosine, cosine], axis=1)
    across = jnp.concatenate([-sine, sine], axis=1)
    turn_ref[:, :rope] = along
    turn_ref[:, rope:] = across
    loads[0].wait()
    queries = query_ref[...].reshape(rows, qk)
    plain = queries[:, :nope]
    head = lax.broadcasted_iota(jnp.int32, (rows, nope), 0) % heads
    spread = jnp.concatenate(
        [jnp.where(head == h, plain, jnp.zeros_like(plain)) for h in range(heads)], axis=1
    )
    for p in range(pairs):
        value = queries[p * heads : (p + 1) * heads, nope:].astype(jnp.float32)
        other = jnp.concatenate([value[:, part:], value[:, :part]], axis=1)
        turned = value * turn_ref[p : p + 1, :rope] + other * turn_ref[p : p + 1, rope:]
        turned = turned.astype(jnp.bfloat16)
        rope_ref[p * heads : (p + 1) * heads, :] = jnp.concatenate([turned, turned], axis=1)
    loads[1].wait()
    fresh = jnp.concatenate([new_ref[s].astype(jnp.float32) for s in range(steps)], axis=0)
    value = fresh[:, latent:]
    other = jnp.concatenate([value[:, part:], value[:, :part]], axis=1)
    turned = value * along + other * across
    fresh = jnp.concatenate(
        [fresh[:, :latent], turned, jnp.zeros_like(turned)], axis=1
    ).astype(jnp.bfloat16)
    loads[2].wait()
    full_ref[...] = jnp.dot(
        spread, w_ref[...].reshape(heads * nope, latent), preferred_element_type=jnp.float32
    ).astype(jnp.bfloat16)
    row = lax.broadcasted_iota(jnp.int32, (16, pairs), 0)
    source = lax.broadcasted_iota(jnp.int32, (16, pairs), 1)
    lane = lax.broadcasted_iota(jnp.int32, (heads, LANES), 1)
    decoder = my_x * dp_count + my_dp
    block = steps * heads
    tiles = latent // LANES
    packed = block * tiles
    for k in range(n):
        group = lax.rem(my_z + k, n)
        seq = jnp.int32(0)
        for m in range(1, seq_dev):
            seq = jnp.where(owner_ref[list_ref[m, decoder]] == group, m, seq)
        at = [
            pl.ds(pl.multiple_of((s * seq_dev + seq) * heads, heads), heads)
            for s in range(steps)
        ]
        for s in range(steps):
            for t in range(tiles):
                first = t * block + s * heads
                out_refs[k][first : first + heads, :] = full_ref[
                    at[s], t * LANES : (t + 1) * LANES
                ]
        for s in range(steps // 2):
            out_refs[k][packed + s * heads : packed + (s + 1) * heads, :] = jnp.where(
                lane < rope, rope_ref[at[s], :], rope_ref[at[s + steps // 2], :]
            )
        if k == 0:
            choose = (source // seq_dev == row) & (source % seq_dev == seq)
            chosen = jnp.dot(
                jnp.where(choose, 1.0, 0.0).astype(jnp.bfloat16),
                fresh,
                preferred_element_type=jnp.float32,
            ).astype(jnp.bfloat16)
            first = packed + block // 2
            length = len_ref[list_ref[seq, decoder]]
            line = lax.broadcasted_iota(jnp.int32, (16, LANES), 0)
            parts = jnp.where(
                line == 8, length // 32, jnp.where(line == 9, length % 32, 0)
            ).astype(jnp.bfloat16)
            for t in range(tiles + 1):
                tile = chosen[:, t * LANES : (t + 1) * LANES]
                if t == tiles:
                    tile = tile + parts
                out_refs[k][first + t * 16 : first + (t + 1) * 16, :] = tile
    total = order_ref.shape[0]
    per = total // n
    row = lax.broadcasted_iota(jnp.int32, (total, 1), 0)
    wanted = jnp.zeros((total, 1), jnp.int32)
    for w in range(n):
        for m in range(seq_dev):
            owner = owner_ref[list_ref[m, w * dp_count + my_dp]]
            first = (lax.rem(my_x - owner + n, n) * n + lax.rem(my_z - w + n, n)) * steps
            here_row = (row // per == w) & (row % seq_dev == m)
            wanted = jnp.where(here_row, first + row % per // seq_dev, wanted)
    source = lax.broadcasted_iota(jnp.int32, (total, total), 1)
    order_ref[...] = jnp.where(source == wanted, 1.0, 0.0).astype(jnp.bfloat16)


def attend_kernel(scale, steps, kv_ref, *refs):
    n = 4
    piece_refs, out_refs, plain_ref, rope_refs = refs[:n], refs[n : 2 * n], refs[2 * n], refs[-2:]
    my_x, _, my_z = here()
    stripes, packed_rows, _ = kv_ref.shape
    block, latent = out_refs[0].shape
    tiles = latent // LANES
    half = packed_rows - 2 * tiles * (packed_rows // (2 * tiles + 1))
    capacity = 2 * half
    heads = block // steps
    packed = tiles * block
    lane = lax.broadcasted_iota(jnp.int32, (block // 2, LANES), 1)
    low = lane < LANES // 2
    for k in range(n):
        at = lax.rem(my_x - my_z - k + 2 * n, n)
        for t in range(tiles):
            plain_ref[at, :, t * LANES : (t + 1) * LANES] = piece_refs[k][
                t * block : (t + 1) * block, :
            ]
        rope = piece_refs[k][packed : packed + block // 2, :]
        swapped = jnp.concatenate([rope[:, LANES // 2 :], rope[:, : LANES // 2]], axis=1)
        blank = jnp.zeros_like(rope)
        rope_refs[0][at, : block // 2, :] = jnp.where(low, rope, blank)
        rope_refs[0][at, block // 2 :, :] = jnp.where(low, swapped, blank)
        rope_refs[1][at, : block // 2, :] = jnp.where(low, blank, swapped)
        rope_refs[1][at, block // 2 :, :] = jnp.where(low, blank, rope)
    plain = plain_ref[...].reshape(n * block, latent)
    sides = [
        jnp.concatenate([plain, ref[...].reshape(n * block, LANES)], axis=1) for ref in rope_refs
    ]
    first = packed + block // 2
    fresh = jnp.concatenate(
        [piece_refs[0][first + t * 16 : first + (t + 1) * 16, :] for t in range(tiles + 1)], axis=1
    )
    parts = fresh[8:10, latent:].astype(jnp.float32).astype(jnp.int32)
    length = parts[:1] * 32 + parts[1:]
    length = jnp.concatenate([length] * (stripes * half // LANES), axis=1)
    rope_keys = kv_ref[:, tiles * capacity :, :].reshape(stripes * half, LANES)
    scores, values = [], []
    for side in range(2):
        parts = [
            kv_ref[:, t * capacity + side * half : t * capacity + (side + 1) * half, :].reshape(
                stripes * half, LANES
            )
            for t in range(tiles)
        ]
        latents = jnp.concatenate(parts, axis=1)
        values.append(latents)
        keys = jnp.concatenate([latents, rope_keys], axis=1)
        score = lax.dot_general(
            sides[side], keys, (((1,), (1,)), ((), ())), preferred_element_type=jnp.float32
        ) * scale
        key_id = lax.broadcasted_iota(jnp.int32, (1, stripes * half), 1)
        position = (side * half + key_id % half) * stripes + key_id // half
        scores.append(jnp.where(position < length, score, -jnp.inf))
    score = lax.dot_general(
        sides[0], fresh, (((1,), (1,)), ((), ())), preferred_element_type=jnp.float32
    ) * scale
    step = lax.broadcasted_iota(jnp.int32, score.shape, 0) // heads % steps
    new_id = lax.broadcasted_iota(jnp.int32, score.shape, 1)
    scores.append(jnp.where(new_id <= step, score, -jnp.inf))
    values.append(fresh[:, :latent])
    peak = jnp.maximum(
        jnp.max(jnp.maximum(scores[0], scores[1]), axis=1, keepdims=True),
        jnp.max(scores[2], axis=1, keepdims=True),
    )
    weights = [jnp.exp(score - peak) for score in scores]
    total = jnp.sum(weights[0] + weights[1], axis=1, keepdims=True) + jnp.sum(
        weights[2], axis=1, keepdims=True
    )
    share = 1.0 / total
    mixed = sum(
        jnp.dot((weight * share).astype(jnp.bfloat16), value, preferred_element_type=jnp.float32)
        for weight, value in zip(weights, values)
    ).astype(jnp.bfloat16)
    for j in range(n):
        out_refs[j][...] = mixed[j * block : (j + 1) * block, :]


def values_kernel(w_ref, *refs):
    n = 4
    piece_refs, out_ref = refs[:n], refs[n]
    heads, latent, width = w_ref.shape
    steps = piece_refs[0].shape[0] // heads
    pieces = [
        piece[...].astype(jnp.float32).reshape(steps, heads, latent) for piece in piece_refs
    ]
    stacked = jnp.concatenate(pieces, axis=0)
    by_head = jnp.swapaxes(stacked, 0, 1).astype(jnp.bfloat16)
    for h in range(heads):
        out_ref[:, h * width : (h + 1) * width] = jnp.dot(
            by_head[h], w_ref[h], preferred_element_type=jnp.float32
        ).astype(jnp.bfloat16)


def project_kernel(order_ref, near_ref, far_ref, *refs):
    n = 4
    piece_refs, out_ref, late_ref, sem = refs[:n], *refs[n:]
    per = piece_refs[0].shape[0]
    columns, early, span = far_ref.shape[1], near_ref.shape[1], 256
    load = pltpu.make_async_copy(far_ref.at[:, early:], late_ref, sem)
    load.start()
    gathered = jnp.concatenate([piece[...] for piece in piece_refs], axis=0)
    ordered = jnp.dot(
        order_ref[...], gathered, preferred_element_type=jnp.float32
    ).astype(jnp.bfloat16)
    for first in range(0, columns, span):
        if first == early:
            load.wait()
        if first < early:
            weight = near_ref[:, first : first + span]
        else:
            weight = late_ref[:, first - early : first - early + span]
        part = jnp.dot(ordered, weight, preferred_element_type=jnp.float32).astype(jnp.bfloat16)
        for w in range(n):
            for z in range(n):
                out_ref[w * n + z, :, first : first + span] = part[w * per : (w + 1) * per, :]


def load_kernel(after_ref, far_ref, near_ref, sem):
    columns = near_ref.shape[-1]
    source = far_ref if columns == far_ref.shape[-1] else far_ref.at[:, :columns]
    load = pltpu.make_async_copy(source, near_ref, sem)
    load.start()
    load.wait()


def bring_near(weight, columns, after, room, name):
    shape = weight.shape[:-1] + (columns,)
    return pl.pallas_call(
        load_kernel,
        out_shape=jax.ShapeDtypeStruct(shape, weight.dtype),
        in_specs=[VMEM, HBM],
        out_specs=VMEM,
        scratch_shapes=[pltpu.SemaphoreType.DMA],
        compiler_params=pltpu.CompilerParams(vmem_limit_bytes=room * MIB),
        cost_estimate=pl.CostEstimate(
            flops=0, bytes_accessed=4 * weight.size, transcendentals=0
        ),
        name=name,
    )(after, weight)


def final_kernel(piece_ref, out_ref):
    n = 4
    steps, seq_dev, _ = out_ref.shape
    columns = piece_ref.shape[2]
    for x in range(n):
        summed = sum(piece_ref[x * n + h].astype(jnp.float32) for h in range(n))
        summed = summed.astype(jnp.bfloat16)
        for s in range(steps):
            out_ref[s, :, x * columns : (x + 1) * columns] = summed[
                s * seq_dev : (s + 1) * seq_dev, :
            ]


def shards(
    prompt_kv, prompt_len, prefill_owner, decode_list, positions, query, new_kv, w_uk, w_uv, w_out
):
    n = lax.axis_size("pf")
    dp_count = lax.axis_size("dp")
    stripes = dp_count * n
    decoders, seq_dev = decode_list.shape
    requests = decoders * seq_dev
    kv_width = prompt_kv.shape[3]
    total = prompt_kv.shape[2]
    capacity = total // decoders
    step_count, _, head_dev, qk_width = query.shape
    latent = w_uk.shape[2]
    rope_width = kv_width - latent
    served = decode_list.T

    packed_rows = capacity * kv_width // LANES
    outgoing = pl.pallas_call(
        functools.partial(pack_kernel, dp_count, n),
        out_shape=jax.ShapeDtypeStruct((stripes, packed_rows, LANES), prompt_kv.dtype),
        in_specs=[HBM] * 3,
        out_specs=HBM,
        scratch_shapes=[
            pltpu.SMEM((requests,), jnp.int32),
            pltpu.SMEM((seq_dev, decoders), jnp.int32),
            pltpu.SMEM((requests,), jnp.int32),
            pltpu.SMEM((decoders,), jnp.int32),
            pltpu.VMEM((kv_width, total), jnp.bfloat16),
            pltpu.VMEM((stripes, packed_rows, LANES), jnp.bfloat16),
            pltpu.SemaphoreType.DMA((2,)),
            pltpu.SemaphoreType.DMA((4,)),
            pltpu.SemaphoreType.DMA,
        ],
        compiler_params=pltpu.CompilerParams(vmem_limit_bytes=FULL),
        name="pack_rows",
    )(prefill_owner, served, prompt_kv[0, 0].T)
    arrived = lax.all_to_all(outgoing, ("dp", "head"), split_axis=0, concat_axis=0, tiled=True)

    ratio = np.arange(rope_width // 2, dtype=np.float64) * 2.0 / rope_width
    frequency = jnp.asarray((ROPE_BASE**-ratio).astype(np.float32))
    rows = step_count * head_dev
    packed_query = rows * latent // LANES + rows // 2
    extra = 16 * (latent // LANES + 1)
    all_rows = n * seq_dev * step_count
    *pieces, order = pl.pallas_call(
        functools.partial(query_kernel, dp_count),
        out_shape=[
            jax.ShapeDtypeStruct((packed_query + (extra if k == 0 else 0), LANES), jnp.bfloat16)
            for k in range(n)
        ]
        + [jax.ShapeDtypeStruct((all_rows, all_rows), jnp.bfloat16)],
        in_specs=[SMEM, SMEM, SMEM, SMEM, VMEM] + [HBM] * 3,
        out_specs=[VMEM] * (n + 1),
        scratch_shapes=[
            pltpu.VMEM((seq_dev * rows, latent), jnp.bfloat16),
            pltpu.VMEM((seq_dev * rows, LANES), jnp.bfloat16),
            pltpu.VMEM((step_count * seq_dev, 2 * rope_width), jnp.float32),
            pltpu.VMEM(query.shape, query.dtype),
            pltpu.VMEM(new_kv.shape, new_kv.dtype),
            pltpu.VMEM(w_uk.shape, w_uk.dtype),
            pltpu.SemaphoreType.DMA((3,)),
        ],
        compiler_params=pltpu.CompilerParams(vmem_limit_bytes=FULL),
        name="project_queries",
    )(prefill_owner, served, prompt_len, positions, frequency[None, :], query, new_kv, w_uk)
    got = [plane(pieces[k], n, lambda x, z, k=k: (z + k, x)) for k in range(n)]

    latent_out = pl.pallas_call(
        functools.partial(attend_kernel, qk_width ** (-0.5), step_count),
        out_shape=[jax.ShapeDtypeStruct((rows, latent), jnp.bfloat16)] * n,
        in_specs=[VMEM] * (n + 1),
        out_specs=[VMEM] * n,
        scratch_shapes=[
            pltpu.VMEM((n, rows, latent), jnp.bfloat16),
            pltpu.VMEM((n, rows, LANES), jnp.bfloat16),
            pltpu.VMEM((n, rows, LANES), jnp.bfloat16),
        ],
        compiler_params=pltpu.CompilerParams(vmem_limit_bytes=12 * MIB),
        name="attend",
    )(arrived, *got)
    w_uv = bring_near(w_uv, w_uv.shape[-1], latent_out[0], 50, "load_w_uv")

    back = [ring(latent_out[j], "head", n, j) for j in range(n)]
    attended = pl.pallas_call(
        values_kernel,
        out_shape=jax.ShapeDtypeStruct(
            (n * step_count, head_dev * w_uv.shape[2]), jnp.bfloat16
        ),
        in_specs=[VMEM] * (n + 1),
        out_specs=VMEM,
        compiler_params=pltpu.CompilerParams(vmem_limit_bytes=12 * MIB),
        name="project_values",
    )(w_uv, *back)
    gathered = [ring(attended, "pf", n, i) for i in range(n)]
    early = 1280
    w_near = bring_near(w_out, early, attended, 44, "load_w_out")
    columns = w_out.shape[1]
    partial_value = pl.pallas_call(
        project_kernel,
        out_shape=jax.ShapeDtypeStruct((n * n, n * step_count, columns), jnp.bfloat16),
        in_specs=[VMEM, VMEM, HBM] + [VMEM] * n,
        out_specs=VMEM,
        scratch_shapes=[
            pltpu.VMEM((w_out.shape[0], columns - early), jnp.bfloat16),
            pltpu.SemaphoreType.DMA,
        ],
        compiler_params=pltpu.CompilerParams(vmem_limit_bytes=44 * MIB),
        name="project_out",
    )(order, w_near, w_out, *gathered)
    final = lax.all_to_all(
        partial_value, ("pf", "head"), split_axis=0, concat_axis=0, tiled=True
    )
    return pl.pallas_call(
        final_kernel,
        out_shape=jax.ShapeDtypeStruct((step_count, seq_dev, n * columns), jnp.bfloat16),
        in_specs=[VMEM],
        out_specs=VMEM,
        compiler_params=pltpu.CompilerParams(vmem_limit_bytes=8 * MIB),
        name="assemble",
    )(final)


def solution(mesh):
    placed = (
        P("pf", ("dp", "head"), None, None),
        P(),
        P(),
        P(),
        P(("pf", "dp")),
        P(None, ("pf", "dp"), "head", None),
        P(None, ("pf", "dp"), None),
        P("head", None, None),
        P("head", None, None),
        P("head", "pf"),
    )
    return jax.shard_map(
        shards, mesh=mesh, in_specs=placed, out_specs=P(None, ("pf", "dp"), None), check_vma=False
    )
```

```python
import functools
import math

import jax
import jax.numpy as jnp
import numpy as np
from jax import lax
from jax.experimental import pallas as pl
from jax.experimental.pallas import tpu as pltpu
from jax.sharding import PartitionSpec as P

ROPE_BASE = 50000.0


def ring(value, axis, count, shift):
    if shift % count == 0:
        return value
    return lax.ppermute(value, axis, [(i, (i + shift) % count) for i in range(count)])


def plane(value, count, target):
    pairs = []
    for x in range(count):
        for z in range(count):
            to_x, to_z = target(x, z)
            pairs.append((x * count + z, (to_x % count) * count + to_z % count))
    return lax.ppermute(value, ("pf", "head"), pairs)


SMEM = pl.BlockSpec(memory_space=pltpu.SMEM)
VMEM = pl.BlockSpec(memory_space=pltpu.VMEM)
HBM = pl.BlockSpec(memory_space=pltpu.HBM)
LANES = 128
MIB = 1024 * 1024
FULL = 125 * MIB // 2


def here():
    return lax.axis_index("pf"), lax.axis_index("dp"), lax.axis_index("head")


def owned_by(list_ref, owner_ref, decoder, group):
    found = list_ref[0, decoder]
    for n in range(1, list_ref.shape[0]):
        request = list_ref[n, decoder]
        found = jnp.where(owner_ref[request] == group, request, found)
    return found


def pack_kernel(dp_count, n, owner_hbm, list_hbm, prompt_ref, out_ref, owner_ref, list_ref,
                rank_ref, target_ref, flat_ref, block_ref, small_sems, in_sems, out_sem):
    seq_dev, decoders = list_ref.shape
    width, total = flat_ref.shape
    capacity = total // decoders
    tiles = width // LANES
    half = capacity // 2
    chunks = in_sems.shape[0]
    span = total // chunks
    slots = decoders // chunks
    my_x, _, _ = here()
    scalars = [
        pltpu.make_async_copy(owner_hbm, owner_ref, small_sems.at[0]),
        pltpu.make_async_copy(list_hbm, list_ref, small_sems.at[1]),
    ]
    for load in scalars:
        load.start()
    loads = []
    for c in range(chunks):
        at = slice(c * span, (c + 1) * span)
        load = pltpu.make_async_copy(prompt_ref.at[:, at], flat_ref.at[:, at], in_sems.at[c])
        load.start()
        loads.append(load)
    for load in scalars:
        load.wait()
    count = jnp.int32(0)
    for request in range(decoders * seq_dev):
        rank_ref[request] = count
        count = count + jnp.where(owner_ref[request] == my_x, 1, 0)
    for decoder in range(decoders):
        slot = rank_ref[owned_by(list_ref, owner_ref, decoder, my_x)]
        target_ref[slot] = decoder % dp_count * n + decoder // dp_count
    for c in range(chunks):
        loads[c].wait()
        rows = flat_ref[: tiles * LANES, c * span : (c + 1) * span].T
        rope = flat_ref[tiles * LANES :, c * span : (c + 1) * span]
        moved = jnp.concatenate([rope[:, half:], rope[:, :half]], axis=1)
        ropes = jnp.concatenate([rope, moved], axis=0).T
        for i in range(slots):
            slot = c * slots + i
            mine = rows[i * capacity : (i + 1) * capacity, :]
            for t in range(tiles):
                block_ref[slot, t * capacity : (t + 1) * capacity, :] = mine[
                    :, t * LANES : (t + 1) * LANES
                ]
            block_ref[slot, tiles * capacity :, :] = ropes[i * capacity : i * capacity + half, :]
            pltpu.make_async_copy(
                block_ref.at[slot], out_ref.at[target_ref[slot]], out_sem
            ).start()
    pltpu.make_async_copy(block_ref, out_ref, out_sem).wait()


def query_kernel(dp_count, owner_ref, list_ref, len_ref, pos_ref, freq_ref, query_hbm, new_hbm,
                 w_hbm, *refs):
    out_refs, order_ref = refs[:4], refs[4]
    full_ref, rope_ref, turn_ref, query_ref, new_ref, w_ref, sems = refs[5:]
    loads = [
        pltpu.make_async_copy(query_hbm, query_ref, sems.at[0]),
        pltpu.make_async_copy(new_hbm, new_ref, sems.at[1]),
        pltpu.make_async_copy(w_hbm, w_ref, sems.at[2]),
    ]
    for load in loads:
        load.start()
    my_x, my_dp, my_z = here()
    n = len(out_refs)
    steps, seq_dev, heads, qk = query_ref.shape
    nope, latent = w_ref.shape[1], w_ref.shape[2]
    rope = qk - nope
    part = rope // 2
    pairs = steps * seq_dev
    rows = pairs * heads
    shape = (pairs, part)
    pair = lax.broadcasted_iota(jnp.int32, shape, 0)
    pos = pair // seq_dev
    for seq in range(seq_dev):
        pos = pos + jnp.where(pair % seq_dev == seq, pos_ref[seq], 0)
    angles = pos.astype(jnp.float32) * freq_ref[...]
    cosine, sine = jnp.cos(angles), jnp.sin(angles)
    along = jnp.concatenate([cosine, cosine], axis=1)
    across = jnp.concatenate([-sine, sine], axis=1)
    turn_ref[:, :rope] = along
    turn_ref[:, rope:] = across
    loads[0].wait()
    queries = query_ref[...].reshape(rows, qk)
    plain = queries[:, :nope]
    head = lax.broadcasted_iota(jnp.int32, (rows, nope), 0) % heads
    spread = jnp.concatenate(
        [jnp.where(head == h, plain, jnp.zeros_like(plain)) for h in range(heads)], axis=1
    )
    for p in range(pairs):
        value = queries[p * heads : (p + 1) * heads, nope:].astype(jnp.float32)
        other = jnp.concatenate([value[:, part:], value[:, :part]], axis=1)
        turned = value * turn_ref[p : p + 1, :rope] + other * turn_ref[p : p + 1, rope:]
        turned = turned.astype(jnp.bfloat16)
        rope_ref[p * heads : (p + 1) * heads, :] = jnp.concatenate([turned, turned], axis=1)
    loads[1].wait()
    fresh = jnp.concatenate([new_ref[s].astype(jnp.float32) for s in range(steps)], axis=0)
    value = fresh[:, latent:]
    other = jnp.concatenate([value[:, part:], value[:, :part]], axis=1)
    turned = value * along + other * across
    fresh = jnp.concatenate(
        [fresh[:, :latent], turned, jnp.zeros_like(turned)], axis=1
    ).astype(jnp.bfloat16)
    loads[2].wait()
    full_ref[...] = jnp.dot(
        spread, w_ref[...].reshape(heads * nope, latent), preferred_element_type=jnp.float32
    ).astype(jnp.bfloat16)
    row = lax.broadcasted_iota(jnp.int32, (16, pairs), 0)
    source = lax.broadcasted_iota(jnp.int32, (16, pairs), 1)
    lane = lax.broadcasted_iota(jnp.int32, (heads, LANES), 1)
    decoder = my_x * dp_count + my_dp
    block = steps * heads
    tiles = latent // LANES
    packed = block * tiles
    for k in range(n):
        group = lax.rem(my_z + k, n)
        seq = jnp.int32(0)
        for m in range(1, seq_dev):
            seq = jnp.where(owner_ref[list_ref[m, decoder]] == group, m, seq)
        at = [
            pl.ds(pl.multiple_of((s * seq_dev + seq) * heads, heads), heads)
            for s in range(steps)
        ]
        for s in range(steps):
            for t in range(tiles):
                first = t * block + s * heads
                out_refs[k][first : first + heads, :] = full_ref[
                    at[s], t * LANES : (t + 1) * LANES
                ]
        for s in range(steps // 2):
            out_refs[k][packed + s * heads : packed + (s + 1) * heads, :] = jnp.where(
                lane < rope, rope_ref[at[s], :], rope_ref[at[s + steps // 2], :]
            )
        if k == 0:
            choose = (source // seq_dev == row) & (source % seq_dev == seq)
            chosen = jnp.dot(
                jnp.where(choose, 1.0, 0.0).astype(jnp.bfloat16),
                fresh,
                preferred_element_type=jnp.float32,
            ).astype(jnp.bfloat16)
            first = packed + block // 2
            length = len_ref[list_ref[seq, decoder]]
            line = lax.broadcasted_iota(jnp.int32, (16, LANES), 0)
            parts = jnp.where(
                line == 8, length // 32, jnp.where(line == 9, length % 32, 0)
            ).astype(jnp.bfloat16)
            for t in range(tiles + 1):
                tile = chosen[:, t * LANES : (t + 1) * LANES]
                if t == tiles:
                    tile = tile + parts
                out_refs[k][first + t * 16 : first + (t + 1) * 16, :] = tile
    total = order_ref.shape[0]
    per = total // n
    row = lax.broadcasted_iota(jnp.int32, (total, 1), 0)
    wanted = jnp.zeros((total, 1), jnp.int32)
    for w in range(n):
        for m in range(seq_dev):
            owner = owner_ref[list_ref[m, w * dp_count + my_dp]]
            first = (lax.rem(my_x - owner + n, n) * n + lax.rem(my_z - w + n, n)) * steps
            here_row = (row // per == w) & (row % seq_dev == m)
            wanted = jnp.where(here_row, first + row % per // seq_dev, wanted)
    source = lax.broadcasted_iota(jnp.int32, (total, total), 1)
    order_ref[...] = jnp.where(source == wanted, 1.0, 0.0).astype(jnp.bfloat16)


def attend_kernel(scale, steps, kv_ref, *refs):
    n = 4
    piece_refs, out_refs, plain_ref, rope_refs = refs[:n], refs[n : 2 * n], refs[2 * n], refs[-2:]
    my_x, _, my_z = here()
    stripes, packed_rows, _ = kv_ref.shape
    block, latent = out_refs[0].shape
    tiles = latent // LANES
    half = packed_rows - 2 * tiles * (packed_rows // (2 * tiles + 1))
    capacity = 2 * half
    heads = block // steps
    packed = tiles * block
    lane = lax.broadcasted_iota(jnp.int32, (block // 2, LANES), 1)
    low = lane < LANES // 2
    for k in range(n):
        at = lax.rem(my_x - my_z - k + 2 * n, n)
        for t in range(tiles):
            plain_ref[at, :, t * LANES : (t + 1) * LANES] = piece_refs[k][
                t * block : (t + 1) * block, :
            ]
        rope = piece_refs[k][packed : packed + block // 2, :]
        swapped = jnp.concatenate([rope[:, LANES // 2 :], rope[:, : LANES // 2]], axis=1)
        blank = jnp.zeros_like(rope)
        rope_refs[0][at, : block // 2, :] = jnp.where(low, rope, blank)
        rope_refs[0][at, block // 2 :, :] = jnp.where(low, swapped, blank)
        rope_refs[1][at, : block // 2, :] = jnp.where(low, blank, swapped)
        rope_refs[1][at, block // 2 :, :] = jnp.where(low, blank, rope)
    plain = plain_ref[...].reshape(n * block, latent)
    sides = [
        jnp.concatenate([plain, ref[...].reshape(n * block, LANES)], axis=1) for ref in rope_refs
    ]
    first = packed + block // 2
    fresh = jnp.concatenate(
        [piece_refs[0][first + t * 16 : first + (t + 1) * 16, :] for t in range(tiles + 1)], axis=1
    )
    parts = fresh[8:10, latent:].astype(jnp.float32).astype(jnp.int32)
    length = parts[:1] * 32 + parts[1:]
    length = jnp.concatenate([length] * (stripes * half // LANES), axis=1)
    rope_keys = kv_ref[:, tiles * capacity :, :].reshape(stripes * half, LANES)
    scores, values = [], []
    for side in range(2):
        parts = [
            kv_ref[:, t * capacity + side * half : t * capacity + (side + 1) * half, :].reshape(
                stripes * half, LANES
            )
            for t in range(tiles)
        ]
        latents = jnp.concatenate(parts, axis=1)
        values.append(latents)
        keys = jnp.concatenate([latents, rope_keys], axis=1)
        score = lax.dot_general(
            sides[side], keys, (((1,), (1,)), ((), ())), preferred_element_type=jnp.float32
        )
        key_id = lax.broadcasted_iota(jnp.int32, (1, stripes * half), 1)
        position = (side * half + key_id % half) * stripes + key_id // half
        scores.append(jnp.where(position < length, score, -jnp.inf))
    score = lax.dot_general(
        sides[0], fresh, (((1,), (1,)), ((), ())), preferred_element_type=jnp.float32
    )
    step = lax.broadcasted_iota(jnp.int32, score.shape, 0) // heads % steps
    new_id = lax.broadcasted_iota(jnp.int32, score.shape, 1)
    scores.append(jnp.where(new_id <= step, score, -jnp.inf))
    values.append(fresh[:, :latent])
    peak = jnp.maximum(
        jnp.max(jnp.maximum(scores[0], scores[1]), axis=1, keepdims=True),
        jnp.max(scores[2], axis=1, keepdims=True),
    )
    turn = scale * math.log2(math.e)
    weights = [jnp.exp2((score - peak) * turn) for score in scores]
    total = jnp.sum(weights[0] + weights[1], axis=1, keepdims=True) + jnp.sum(
        weights[2], axis=1, keepdims=True
    )
    share = 1.0 / total
    mixed = sum(
        jnp.dot((weight * share).astype(jnp.bfloat16), value, preferred_element_type=jnp.float32)
        for weight, value in zip(weights, values)
    ).astype(jnp.bfloat16)
    for j in range(n):
        out_refs[j][...] = mixed[j * block : (j + 1) * block, :]


def values_kernel(w_ref, *refs):
    n = 4
    piece_refs, out_ref = refs[:n], refs[n]
    heads, latent, width = w_ref.shape
    steps = piece_refs[0].shape[0] // heads
    pieces = [
        piece[...].astype(jnp.float32).reshape(steps, heads, latent) for piece in piece_refs
    ]
    stacked = jnp.concatenate(pieces, axis=0)
    by_head = jnp.swapaxes(stacked, 0, 1).astype(jnp.bfloat16)
    for h in range(heads):
        out_ref[:, h * width : (h + 1) * width] = jnp.dot(
            by_head[h], w_ref[h], preferred_element_type=jnp.float32
        ).astype(jnp.bfloat16)


def project_kernel(order_ref, w_ref, *refs):
    n = 4
    piece_refs, out_ref = refs[:n], refs[n]
    per = piece_refs[0].shape[0]
    columns, span = w_ref.shape[1], 256
    gathered = jnp.concatenate([piece[...] for piece in piece_refs], axis=0)
    ordered = jnp.dot(
        order_ref[...], gathered, preferred_element_type=jnp.float32
    ).astype(jnp.bfloat16)
    for first in range(0, columns, span):
        part = jnp.dot(
            ordered, w_ref[:, first : first + span], preferred_element_type=jnp.float32
        ).astype(jnp.bfloat16)
        for w in range(n):
            for z in range(n):
                out_ref[w * n + z, :, first : first + span] = part[w * per : (w + 1) * per, :]


def load_kernel(after_ref, far_ref, near_ref, sem):
    load = pltpu.make_async_copy(far_ref, near_ref, sem)
    load.start()
    load.wait()


def bring_near(weight, after, room, name):
    return pl.pallas_call(
        load_kernel,
        out_shape=jax.ShapeDtypeStruct(weight.shape, weight.dtype),
        in_specs=[VMEM, HBM],
        out_specs=VMEM,
        scratch_shapes=[pltpu.SemaphoreType.DMA],
        compiler_params=pltpu.CompilerParams(vmem_limit_bytes=room * MIB),
        cost_estimate=pl.CostEstimate(
            flops=0, bytes_accessed=4 * weight.size, transcendentals=0
        ),
        name=name,
    )(after, weight)


def final_kernel(piece_ref, out_ref):
    n = 4
    steps, seq_dev, _ = out_ref.shape
    columns = piece_ref.shape[2]
    for x in range(n):
        summed = sum(piece_ref[x * n + h].astype(jnp.float32) for h in range(n))
        summed = summed.astype(jnp.bfloat16)
        for s in range(steps):
            out_ref[s, :, x * columns : (x + 1) * columns] = summed[
                s * seq_dev : (s + 1) * seq_dev, :
            ]


def shards(
    prompt_kv, prompt_len, prefill_owner, decode_list, positions, query, new_kv, w_uk, w_uv, w_out
):
    n = lax.axis_size("pf")
    dp_count = lax.axis_size("dp")
    stripes = dp_count * n
    decoders, seq_dev = decode_list.shape
    requests = decoders * seq_dev
    kv_width = prompt_kv.shape[3]
    total = prompt_kv.shape[2]
    capacity = total // decoders
    step_count, _, head_dev, qk_width = query.shape
    latent = w_uk.shape[2]
    rope_width = kv_width - latent
    served = decode_list.T

    packed_rows = capacity * kv_width // LANES
    outgoing = pl.pallas_call(
        functools.partial(pack_kernel, dp_count, n),
        out_shape=jax.ShapeDtypeStruct((stripes, packed_rows, LANES), prompt_kv.dtype),
        in_specs=[HBM] * 3,
        out_specs=HBM,
        scratch_shapes=[
            pltpu.SMEM((requests,), jnp.int32),
            pltpu.SMEM((seq_dev, decoders), jnp.int32),
            pltpu.SMEM((requests,), jnp.int32),
            pltpu.SMEM((decoders,), jnp.int32),
            pltpu.VMEM((kv_width, total), jnp.bfloat16),
            pltpu.VMEM((stripes, packed_rows, LANES), jnp.bfloat16),
            pltpu.SemaphoreType.DMA((2,)),
            pltpu.SemaphoreType.DMA((4,)),
            pltpu.SemaphoreType.DMA,
        ],
        compiler_params=pltpu.CompilerParams(vmem_limit_bytes=FULL),
        name="pack_rows",
    )(prefill_owner, served, prompt_kv[0, 0].T)
    arrived = lax.all_to_all(outgoing, ("dp", "head"), split_axis=0, concat_axis=0, tiled=True)

    ratio = np.arange(rope_width // 2, dtype=np.float64) * 2.0 / rope_width
    frequency = jnp.asarray((ROPE_BASE**-ratio).astype(np.float32))
    rows = step_count * head_dev
    packed_query = rows * latent // LANES + rows // 2
    extra = 16 * (latent // LANES + 1)
    all_rows = n * seq_dev * step_count
    *pieces, order = pl.pallas_call(
        functools.partial(query_kernel, dp_count),
        out_shape=[
            jax.ShapeDtypeStruct((packed_query + (extra if k == 0 else 0), LANES), jnp.bfloat16)
            for k in range(n)
        ]
        + [jax.ShapeDtypeStruct((all_rows, all_rows), jnp.bfloat16)],
        in_specs=[SMEM, SMEM, SMEM, SMEM, VMEM] + [HBM] * 3,
        out_specs=[VMEM] * (n + 1),
        scratch_shapes=[
            pltpu.VMEM((seq_dev * rows, latent), jnp.bfloat16),
            pltpu.VMEM((seq_dev * rows, LANES), jnp.bfloat16),
            pltpu.VMEM((step_count * seq_dev, 2 * rope_width), jnp.float32),
            pltpu.VMEM(query.shape, query.dtype),
            pltpu.VMEM(new_kv.shape, new_kv.dtype),
            pltpu.VMEM(w_uk.shape, w_uk.dtype),
            pltpu.SemaphoreType.DMA((3,)),
        ],
        compiler_params=pltpu.CompilerParams(vmem_limit_bytes=FULL),
        name="project_queries",
    )(prefill_owner, served, prompt_len, positions, frequency[None, :], query, new_kv, w_uk)
    got = [plane(pieces[k], n, lambda x, z, k=k: (z + k, x)) for k in range(n)]

    latent_out = pl.pallas_call(
        functools.partial(attend_kernel, qk_width ** (-0.5), step_count),
        out_shape=[jax.ShapeDtypeStruct((rows, latent), jnp.bfloat16)] * n,
        in_specs=[VMEM] * (n + 1),
        out_specs=[VMEM] * n,
        scratch_shapes=[
            pltpu.VMEM((n, rows, latent), jnp.bfloat16),
            pltpu.VMEM((n, rows, LANES), jnp.bfloat16),
            pltpu.VMEM((n, rows, LANES), jnp.bfloat16),
        ],
        compiler_params=pltpu.CompilerParams(vmem_limit_bytes=12 * MIB),
        name="attend",
    )(arrived, *got)
    w_uv = bring_near(w_uv, latent_out[0], 50, "load_w_uv")

    back = [ring(latent_out[j], "head", n, j) for j in range(n)]
    attended = pl.pallas_call(
        values_kernel,
        out_shape=jax.ShapeDtypeStruct(
            (n * step_count, head_dev * w_uv.shape[2]), jnp.bfloat16
        ),
        in_specs=[VMEM] * (n + 1),
        out_specs=VMEM,
        compiler_params=pltpu.CompilerParams(vmem_limit_bytes=12 * MIB),
        name="project_values",
    )(w_uv, *back)
    gathered = [ring(attended, "pf", n, i) for i in range(n)]
    w_out = bring_near(w_out, attended, 43, "load_w_out")
    columns = w_out.shape[1]
    partial_value = pl.pallas_call(
        project_kernel,
        out_shape=jax.ShapeDtypeStruct((n * n, n * step_count, columns), jnp.bfloat16),
        in_specs=[VMEM] * (n + 2),
        out_specs=VMEM,
        compiler_params=pltpu.CompilerParams(vmem_limit_bytes=12 * MIB),
        name="project_out",
    )(order, w_out, *gathered)
    final = lax.all_to_all(
        partial_value, ("pf", "head"), split_axis=0, concat_axis=0, tiled=True
    )
    return pl.pallas_call(
        final_kernel,
        out_shape=jax.ShapeDtypeStruct((step_count, seq_dev, n * columns), jnp.bfloat16),
        in_specs=[VMEM],
        out_specs=VMEM,
        compiler_params=pltpu.CompilerParams(vmem_limit_bytes=8 * MIB),
        name="assemble",
    )(final)


def solution(mesh):
    placed = (
        P("pf", ("dp", "head"), None, None),
        P(),
        P(),
        P(),
        P(("pf", "dp")),
        P(None, ("pf", "dp"), "head", None),
        P(None, ("pf", "dp"), None),
        P("head", None, None),
        P("head", None, None),
        P("head", "pf"),
    )
    return jax.shard_map(
        shards, mesh=mesh, in_specs=placed, out_specs=P(None, ("pf", "dp"), None), check_vma=False
    )
```

```python
import functools
import math

import jax
import jax.numpy as jnp
import numpy as np
from jax import lax
from jax.experimental import pallas as pl
from jax.experimental.pallas import tpu as pltpu
from jax.sharding import PartitionSpec as P

ROPE_BASE = 50000.0


def ring(value, axis, count, shift):
    if shift % count == 0:
        return value
    return lax.ppermute(value, axis, [(i, (i + shift) % count) for i in range(count)])


def plane(value, count, target):
    pairs = []
    for x in range(count):
        for z in range(count):
            to_x, to_z = target(x, z)
            pairs.append((x * count + z, (to_x % count) * count + to_z % count))
    return lax.ppermute(value, ("pf", "head"), pairs)


SMEM = pl.BlockSpec(memory_space=pltpu.SMEM)
VMEM = pl.BlockSpec(memory_space=pltpu.VMEM)
HBM = pl.BlockSpec(memory_space=pltpu.HBM)
LANES = 128
MIB = 1024 * 1024
FULL = 125 * MIB // 2


def here():
    return lax.axis_index("pf"), lax.axis_index("dp"), lax.axis_index("head")


def owned_by(list_ref, owner_ref, decoder, group):
    found = list_ref[0, decoder]
    for n in range(1, list_ref.shape[0]):
        request = list_ref[n, decoder]
        found = jnp.where(owner_ref[request] == group, request, found)
    return found


def pack_kernel(dp_count, n, owner_hbm, list_hbm, prompt_ref, out_ref, owner_ref, list_ref,
                rank_ref, target_ref, flat_ref, block_ref, small_sems, in_sems, out_sem):
    seq_dev, decoders = list_ref.shape
    width, total = flat_ref.shape
    capacity = total // decoders
    tiles = width // LANES
    half = capacity // 2
    chunks = in_sems.shape[0]
    span = total // chunks
    slots = decoders // chunks
    my_x, _, _ = here()
    scalars = [
        pltpu.make_async_copy(owner_hbm, owner_ref, small_sems.at[0]),
        pltpu.make_async_copy(list_hbm, list_ref, small_sems.at[1]),
    ]
    for load in scalars:
        load.start()
    loads = []
    for c in range(chunks):
        at = slice(c * span, (c + 1) * span)
        load = pltpu.make_async_copy(prompt_ref.at[:, at], flat_ref.at[:, at], in_sems.at[c])
        load.start()
        loads.append(load)
    for load in scalars:
        load.wait()
    count = jnp.int32(0)
    for request in range(decoders * seq_dev):
        rank_ref[request] = count
        count = count + jnp.where(owner_ref[request] == my_x, 1, 0)
    for decoder in range(decoders):
        slot = rank_ref[owned_by(list_ref, owner_ref, decoder, my_x)]
        target_ref[slot] = decoder % dp_count * n + decoder // dp_count
    for c in range(chunks):
        loads[c].wait()
        rows = flat_ref[: tiles * LANES, c * span : (c + 1) * span].T
        rope = flat_ref[tiles * LANES :, c * span : (c + 1) * span]
        moved = jnp.concatenate([rope[:, half:], rope[:, :half]], axis=1)
        ropes = jnp.concatenate([rope, moved], axis=0).T
        for i in range(slots):
            slot = c * slots + i
            mine = rows[i * capacity : (i + 1) * capacity, :]
            for t in range(tiles):
                block_ref[slot, t * capacity : (t + 1) * capacity, :] = mine[
                    :, t * LANES : (t + 1) * LANES
                ]
            block_ref[slot, tiles * capacity :, :] = ropes[i * capacity : i * capacity + half, :]
            pltpu.make_async_copy(
                block_ref.at[slot], out_ref.at[target_ref[slot]], out_sem
            ).start()
    pltpu.make_async_copy(block_ref, out_ref, out_sem).wait()


def query_kernel(dp_count, owner_ref, list_ref, len_ref, pos_ref, freq_ref, query_hbm, new_hbm,
                 w_hbm, *refs):
    out_refs, order_ref = refs[:4], refs[4]
    full_ref, rope_ref, turn_ref, query_ref, new_ref, w_ref, sems = refs[5:]
    loads = [
        pltpu.make_async_copy(query_hbm, query_ref, sems.at[0]),
        pltpu.make_async_copy(new_hbm, new_ref, sems.at[1]),
        pltpu.make_async_copy(w_hbm, w_ref, sems.at[2]),
    ]
    for load in loads:
        load.start()
    my_x, my_dp, my_z = here()
    n = len(out_refs)
    steps, seq_dev, heads, qk = query_ref.shape
    nope, latent = w_ref.shape[1], w_ref.shape[2]
    rope = qk - nope
    part = rope // 2
    pairs = steps * seq_dev
    rows = pairs * heads
    shape = (pairs, part)
    pair = lax.broadcasted_iota(jnp.int32, shape, 0)
    pos = pair // seq_dev
    for seq in range(seq_dev):
        pos = pos + jnp.where(pair % seq_dev == seq, pos_ref[seq], 0)
    angles = pos.astype(jnp.float32) * freq_ref[...]
    cosine, sine = jnp.cos(angles), jnp.sin(angles)
    along = jnp.concatenate([cosine, cosine], axis=1)
    across = jnp.concatenate([-sine, sine], axis=1)
    turn_ref[:, :rope] = along
    turn_ref[:, rope:] = across
    loads[0].wait()
    queries = query_ref[...].reshape(rows, qk)
    plain = queries[:, :nope]
    head = lax.broadcasted_iota(jnp.int32, (rows, nope), 0) % heads
    spread = jnp.concatenate(
        [jnp.where(head == h, plain, jnp.zeros_like(plain)) for h in range(heads)], axis=1
    )
    for p in range(pairs):
        value = queries[p * heads : (p + 1) * heads, nope:].astype(jnp.float32)
        other = jnp.concatenate([value[:, part:], value[:, :part]], axis=1)
        turned = value * turn_ref[p : p + 1, :rope] + other * turn_ref[p : p + 1, rope:]
        turned = turned.astype(jnp.bfloat16)
        rope_ref[p * heads : (p + 1) * heads, :] = jnp.concatenate([turned, turned], axis=1)
    loads[1].wait()
    fresh = jnp.concatenate([new_ref[s].astype(jnp.float32) for s in range(steps)], axis=0)
    value = fresh[:, latent:]
    other = jnp.concatenate([value[:, part:], value[:, :part]], axis=1)
    turned = value * along + other * across
    fresh = jnp.concatenate(
        [fresh[:, :latent], turned, jnp.zeros_like(turned)], axis=1
    ).astype(jnp.bfloat16)
    loads[2].wait()
    full_ref[...] = jnp.dot(
        spread, w_ref[...].reshape(heads * nope, latent), preferred_element_type=jnp.float32
    ).astype(jnp.bfloat16)
    row = lax.broadcasted_iota(jnp.int32, (16, pairs), 0)
    source = lax.broadcasted_iota(jnp.int32, (16, pairs), 1)
    lane = lax.broadcasted_iota(jnp.int32, (heads, LANES), 1)
    decoder = my_x * dp_count + my_dp
    block = steps * heads
    tiles = latent // LANES
    packed = block * tiles
    for k in range(n):
        group = lax.rem(my_z + k, n)
        seq = jnp.int32(0)
        for m in range(1, seq_dev):
            seq = jnp.where(owner_ref[list_ref[m, decoder]] == group, m, seq)
        at = [
            pl.ds(pl.multiple_of((s * seq_dev + seq) * heads, heads), heads)
            for s in range(steps)
        ]
        for s in range(steps):
            for t in range(tiles):
                first = t * block + s * heads
                out_refs[k][first : first + heads, :] = full_ref[
                    at[s], t * LANES : (t + 1) * LANES
                ]
        for s in range(steps // 2):
            out_refs[k][packed + s * heads : packed + (s + 1) * heads, :] = jnp.where(
                lane < rope, rope_ref[at[s], :], rope_ref[at[s + steps // 2], :]
            )
        if k == 0:
            choose = (source // seq_dev == row) & (source % seq_dev == seq)
            chosen = jnp.dot(
                jnp.where(choose, 1.0, 0.0).astype(jnp.bfloat16),
                fresh,
                preferred_element_type=jnp.float32,
            ).astype(jnp.bfloat16)
            first = packed + block // 2
            length = len_ref[list_ref[seq, decoder]]
            line = lax.broadcasted_iota(jnp.int32, (16, LANES), 0)
            parts = jnp.where(
                line == 8, length // 32, jnp.where(line == 9, length % 32, 0)
            ).astype(jnp.bfloat16)
            for t in range(tiles + 1):
                tile = chosen[:, t * LANES : (t + 1) * LANES]
                if t == tiles:
                    tile = tile + parts
                out_refs[k][first + t * 16 : first + (t + 1) * 16, :] = tile
    total = order_ref.shape[0]
    per = total // n
    row = lax.broadcasted_iota(jnp.int32, (total, 1), 0)
    wanted = jnp.zeros((total, 1), jnp.int32)
    for w in range(n):
        for m in range(seq_dev):
            owner = owner_ref[list_ref[m, w * dp_count + my_dp]]
            first = (lax.rem(my_x - owner + n, n) * n + lax.rem(my_z - w + n, n)) * steps
            here_row = (row // per == w) & (row % seq_dev == m)
            wanted = jnp.where(here_row, first + row % per // seq_dev, wanted)
    source = lax.broadcasted_iota(jnp.int32, (total, total), 1)
    order_ref[...] = jnp.where(source == wanted, 1.0, 0.0).astype(jnp.bfloat16)


def attend_kernel(scale, steps, kv_ref, *refs):
    n = 4
    piece_refs, out_refs, plain_ref, rope_refs = refs[:n], refs[n : 2 * n], refs[2 * n], refs[-2:]
    my_x, _, my_z = here()
    stripes, packed_rows, _ = kv_ref.shape
    block, latent = out_refs[0].shape
    tiles = latent // LANES
    half = packed_rows - 2 * tiles * (packed_rows // (2 * tiles + 1))
    capacity = 2 * half
    heads = block // steps
    packed = tiles * block
    lane = lax.broadcasted_iota(jnp.int32, (block // 2, LANES), 1)
    low = lane < LANES // 2
    for k in range(n):
        at = lax.rem(my_x - my_z - k + 2 * n, n)
        for t in range(tiles):
            plain_ref[at, :, t * LANES : (t + 1) * LANES] = piece_refs[k][
                t * block : (t + 1) * block, :
            ]
        rope = piece_refs[k][packed : packed + block // 2, :]
        swapped = jnp.concatenate([rope[:, LANES // 2 :], rope[:, : LANES // 2]], axis=1)
        blank = jnp.zeros_like(rope)
        rope_refs[0][at, : block // 2, :] = jnp.where(low, rope, blank)
        rope_refs[0][at, block // 2 :, :] = jnp.where(low, swapped, blank)
        rope_refs[1][at, : block // 2, :] = jnp.where(low, blank, swapped)
        rope_refs[1][at, block // 2 :, :] = jnp.where(low, blank, rope)
    plain = plain_ref[...].reshape(n * block, latent)
    sides = [
        jnp.concatenate([plain, ref[...].reshape(n * block, LANES)], axis=1) for ref in rope_refs
    ]
    first = packed + block // 2
    fresh = jnp.concatenate(
        [piece_refs[0][first + t * 16 : first + (t + 1) * 16, :] for t in range(tiles + 1)], axis=1
    )
    parts = fresh[8:10, latent:].astype(jnp.float32).astype(jnp.int32)
    length = parts[:1] * 32 + parts[1:]
    length = jnp.concatenate([length] * (stripes * half // LANES), axis=1)
    rope_keys = kv_ref[:, tiles * capacity :, :].reshape(stripes * half, LANES)
    scores, values = [], []
    for side in range(2):
        parts = [
            kv_ref[:, t * capacity + side * half : t * capacity + (side + 1) * half, :].reshape(
                stripes * half, LANES
            )
            for t in range(tiles)
        ]
        latents = jnp.concatenate(parts, axis=1)
        values.append(latents)
        keys = jnp.concatenate([latents, rope_keys], axis=1)
        score = lax.dot_general(
            sides[side], keys, (((1,), (1,)), ((), ())), preferred_element_type=jnp.float32
        )
        key_id = lax.broadcasted_iota(jnp.int32, (1, stripes * half), 1)
        position = (side * half + key_id % half) * stripes + key_id // half
        scores.append(jnp.where(position < length, score, -jnp.inf))
    score = lax.dot_general(
        sides[0], fresh, (((1,), (1,)), ((), ())), preferred_element_type=jnp.float32
    )
    step = lax.broadcasted_iota(jnp.int32, score.shape, 0) // heads % steps
    new_id = lax.broadcasted_iota(jnp.int32, score.shape, 1)
    scores.append(jnp.where(new_id <= step, score, -jnp.inf))
    values.append(fresh[:, :latent])
    peak = jnp.maximum(
        jnp.max(jnp.maximum(scores[0], scores[1]), axis=1, keepdims=True),
        jnp.max(scores[2], axis=1, keepdims=True),
    )
    turn = scale * math.log2(math.e)
    weights = [jnp.exp2((score - peak) * turn) for score in scores]
    total = jnp.sum(weights[0] + weights[1], axis=1, keepdims=True) + jnp.sum(
        weights[2], axis=1, keepdims=True
    )
    share = 1.0 / total
    mixed = sum(
        jnp.dot((weight * share).astype(jnp.bfloat16), value, preferred_element_type=jnp.float32)
        for weight, value in zip(weights, values)
    ).astype(jnp.bfloat16)
    for j in range(n):
        out_refs[j][...] = mixed[j * block : (j + 1) * block, :]


def values_kernel(w_ref, *refs):
    n = 4
    piece_refs, out_ref = refs[:n], refs[n]
    heads, latent, width = w_ref.shape
    steps = piece_refs[0].shape[0] // heads
    pieces = [
        piece[...].astype(jnp.float32).reshape(steps, heads, latent) for piece in piece_refs
    ]
    stacked = jnp.concatenate(pieces, axis=0)
    by_head = jnp.swapaxes(stacked, 0, 1).astype(jnp.bfloat16)
    for h in range(heads):
        out_ref[:, h * width : (h + 1) * width] = jnp.dot(
            by_head[h], w_ref[h], preferred_element_type=jnp.float32
        ).astype(jnp.bfloat16)


def project_kernel(order_ref, w_ref, *refs):
    n = 4
    piece_refs, out_ref = refs[:n], refs[n]
    per = piece_refs[0].shape[0]
    columns, span = w_ref.shape[1], 256
    gathered = jnp.concatenate([piece[...] for piece in piece_refs], axis=0)
    ordered = jnp.dot(
        order_ref[...], gathered, preferred_element_type=jnp.float32
    ).astype(jnp.bfloat16)
    for first in range(0, columns, span):
        part = jnp.dot(
            ordered, w_ref[:, first : first + span], preferred_element_type=jnp.float32
        ).astype(jnp.bfloat16)
        for w in range(n):
            for z in range(n):
                out_ref[w * n + z, :, first : first + span] = part[w * per : (w + 1) * per, :]


def load_kernel(after_ref, far_ref, near_ref, sem):
    load = pltpu.make_async_copy(far_ref, near_ref, sem)
    load.start()
    load.wait()


def bring_near(weight, after, room, name):
    return pl.pallas_call(
        load_kernel,
        out_shape=jax.ShapeDtypeStruct(weight.shape, weight.dtype),
        in_specs=[VMEM, HBM],
        out_specs=VMEM,
        scratch_shapes=[pltpu.SemaphoreType.DMA],
        compiler_params=pltpu.CompilerParams(vmem_limit_bytes=room * MIB),
        cost_estimate=pl.CostEstimate(
            flops=0, bytes_accessed=4 * weight.size, transcendentals=0
        ),
        name=name,
    )(after, weight)


def final_kernel(piece_ref, out_ref):
    n = 4
    steps, seq_dev, _ = out_ref.shape
    columns = piece_ref.shape[2]
    for x in range(n):
        summed = sum(piece_ref[x * n + h].astype(jnp.float32) for h in range(n))
        summed = summed.astype(jnp.bfloat16)
        for s in range(steps):
            out_ref[s, :, x * columns : (x + 1) * columns] = summed[
                s * seq_dev : (s + 1) * seq_dev, :
            ]


def shards(
    prompt_kv, prompt_len, prefill_owner, decode_list, positions, query, new_kv, w_uk, w_uv, w_out
):
    n = lax.axis_size("pf")
    dp_count = lax.axis_size("dp")
    stripes = dp_count * n
    decoders, seq_dev = decode_list.shape
    requests = decoders * seq_dev
    kv_width = prompt_kv.shape[3]
    total = prompt_kv.shape[2]
    capacity = total // decoders
    step_count, _, head_dev, qk_width = query.shape
    latent = w_uk.shape[2]
    rope_width = kv_width - latent
    served = decode_list.T

    packed_rows = capacity * kv_width // LANES
    outgoing = pl.pallas_call(
        functools.partial(pack_kernel, dp_count, n),
        out_shape=jax.ShapeDtypeStruct((stripes, packed_rows, LANES), prompt_kv.dtype),
        in_specs=[HBM] * 3,
        out_specs=HBM,
        scratch_shapes=[
            pltpu.SMEM((requests,), jnp.int32),
            pltpu.SMEM((seq_dev, decoders), jnp.int32),
            pltpu.SMEM((requests,), jnp.int32),
            pltpu.SMEM((decoders,), jnp.int32),
            pltpu.VMEM((kv_width, total), jnp.bfloat16),
            pltpu.VMEM((stripes, packed_rows, LANES), jnp.bfloat16),
            pltpu.SemaphoreType.DMA((2,)),
            pltpu.SemaphoreType.DMA((2,)),
            pltpu.SemaphoreType.DMA,
        ],
        compiler_params=pltpu.CompilerParams(vmem_limit_bytes=FULL),
        name="pack_rows",
    )(prefill_owner, served, prompt_kv[0, 0].T)
    arrived = lax.all_to_all(outgoing, ("dp", "head"), split_axis=0, concat_axis=0, tiled=True)

    ratio = np.arange(rope_width // 2, dtype=np.float64) * 2.0 / rope_width
    frequency = jnp.asarray((ROPE_BASE**-ratio).astype(np.float32))
    rows = step_count * head_dev
    packed_query = rows * latent // LANES + rows // 2
    extra = 16 * (latent // LANES + 1)
    all_rows = n * seq_dev * step_count
    *pieces, order = pl.pallas_call(
        functools.partial(query_kernel, dp_count),
        out_shape=[
            jax.ShapeDtypeStruct((packed_query + (extra if k == 0 else 0), LANES), jnp.bfloat16)
            for k in range(n)
        ]
        + [jax.ShapeDtypeStruct((all_rows, all_rows), jnp.bfloat16)],
        in_specs=[SMEM, SMEM, SMEM, SMEM, VMEM] + [HBM] * 3,
        out_specs=[VMEM] * (n + 1),
        scratch_shapes=[
            pltpu.VMEM((seq_dev * rows, latent), jnp.bfloat16),
            pltpu.VMEM((seq_dev * rows, LANES), jnp.bfloat16),
            pltpu.VMEM((step_count * seq_dev, 2 * rope_width), jnp.float32),
            pltpu.VMEM(query.shape, query.dtype),
            pltpu.VMEM(new_kv.shape, new_kv.dtype),
            pltpu.VMEM(w_uk.shape, w_uk.dtype),
            pltpu.SemaphoreType.DMA((3,)),
        ],
        compiler_params=pltpu.CompilerParams(vmem_limit_bytes=FULL),
        name="project_queries",
    )(prefill_owner, served, prompt_len, positions, frequency[None, :], query, new_kv, w_uk)
    got = [plane(pieces[k], n, lambda x, z, k=k: (z + k, x)) for k in range(n)]

    latent_out = pl.pallas_call(
        functools.partial(attend_kernel, qk_width ** (-0.5), step_count),
        out_shape=[jax.ShapeDtypeStruct((rows, latent), jnp.bfloat16)] * n,
        in_specs=[VMEM] * (n + 1),
        out_specs=[VMEM] * n,
        scratch_shapes=[
            pltpu.VMEM((n, rows, latent), jnp.bfloat16),
            pltpu.VMEM((n, rows, LANES), jnp.bfloat16),
            pltpu.VMEM((n, rows, LANES), jnp.bfloat16),
        ],
        compiler_params=pltpu.CompilerParams(vmem_limit_bytes=12 * MIB),
        name="attend",
    )(arrived, *got)
    w_uv = bring_near(w_uv, latent_out[0], 50, "load_w_uv")

    back = [ring(latent_out[j], "head", n, j) for j in range(n)]
    attended = pl.pallas_call(
        values_kernel,
        out_shape=jax.ShapeDtypeStruct(
            (n * step_count, head_dev * w_uv.shape[2]), jnp.bfloat16
        ),
        in_specs=[VMEM] * (n + 1),
        out_specs=VMEM,
        compiler_params=pltpu.CompilerParams(vmem_limit_bytes=12 * MIB),
        name="project_values",
    )(w_uv, *back)
    gathered = [ring(attended, "pf", n, i) for i in range(n)]
    w_out = bring_near(w_out, attended, 43, "load_w_out")
    columns = w_out.shape[1]
    partial_value = pl.pallas_call(
        project_kernel,
        out_shape=jax.ShapeDtypeStruct((n * n, n * step_count, columns), jnp.bfloat16),
        in_specs=[VMEM] * (n + 2),
        out_specs=VMEM,
        compiler_params=pltpu.CompilerParams(vmem_limit_bytes=12 * MIB),
        name="project_out",
    )(order, w_out, *gathered)
    final = lax.all_to_all(
        partial_value, ("pf", "head"), split_axis=0, concat_axis=0, tiled=True
    )
    return pl.pallas_call(
        final_kernel,
        out_shape=jax.ShapeDtypeStruct((step_count, seq_dev, n * columns), jnp.bfloat16),
        in_specs=[VMEM],
        out_specs=VMEM,
        compiler_params=pltpu.CompilerParams(vmem_limit_bytes=8 * MIB),
        name="assemble",
    )(final)


def solution(mesh):
    placed = (
        P("pf", ("dp", "head"), None, None),
        P(),
        P(),
        P(),
        P(("pf", "dp")),
        P(None, ("pf", "dp"), "head", None),
        P(None, ("pf", "dp"), None),
        P("head", None, None),
        P("head", None, None),
        P("head", "pf"),
    )
    return jax.shard_map(
        shards, mesh=mesh, in_specs=placed, out_specs=P(None, ("pf", "dp"), None), check_vma=False
    )
```

```python
import functools
import math

import jax
import jax.numpy as jnp
import numpy as np
from jax import lax
from jax.experimental import pallas as pl
from jax.experimental.pallas import tpu as pltpu
from jax.sharding import PartitionSpec as P

ROPE_BASE = 50000.0


def ring(value, axis, count, shift):
    if shift % count == 0:
        return value
    return lax.ppermute(value, axis, [(i, (i + shift) % count) for i in range(count)])


def swap(value, axis, count, bits):
    return lax.ppermute(value, axis, [(i, i ^ bits) for i in range(count)])


def plane(value, count, target):
    pairs = []
    for x in range(count):
        for z in range(count):
            to_x, to_z = target(x, z)
            pairs.append((x * count + z, to_x * count + to_z))
    return lax.ppermute(value, ("pf", "head"), pairs)


SMEM = pl.BlockSpec(memory_space=pltpu.SMEM)
VMEM = pl.BlockSpec(memory_space=pltpu.VMEM)
HBM = pl.BlockSpec(memory_space=pltpu.HBM)
LANES = 128
MIB = 1024 * 1024
FULL = 125 * MIB // 2


def here():
    return lax.axis_index("pf"), lax.axis_index("dp"), lax.axis_index("head")


def owned_by(list_ref, owner_ref, decoder, group):
    found = list_ref[0, decoder]
    for n in range(1, list_ref.shape[0]):
        request = list_ref[n, decoder]
        found = jnp.where(owner_ref[request] == group, request, found)
    return found


def pack_kernel(dp_count, n, owner_hbm, list_hbm, prompt_ref, out_ref, owner_ref, list_ref,
                rank_ref, target_ref, flat_ref, block_ref, small_sems, in_sems, out_sem):
    seq_dev, decoders = list_ref.shape
    width, total = flat_ref.shape
    capacity = total // decoders
    tiles = width // LANES
    half = capacity // 2
    chunks = in_sems.shape[0]
    span = total // chunks
    slots = decoders // chunks
    my_x, _, _ = here()
    scalars = [
        pltpu.make_async_copy(owner_hbm, owner_ref, small_sems.at[0]),
        pltpu.make_async_copy(list_hbm, list_ref, small_sems.at[1]),
    ]
    for load in scalars:
        load.start()
    loads = []
    for c in range(chunks):
        at = slice(c * span, (c + 1) * span)
        load = pltpu.make_async_copy(prompt_ref.at[:, at], flat_ref.at[:, at], in_sems.at[c])
        load.start()
        loads.append(load)
    for load in scalars:
        load.wait()
    count = jnp.int32(0)
    for request in range(decoders * seq_dev):
        rank_ref[request] = count
        count = count + jnp.where(owner_ref[request] == my_x, 1, 0)
    for decoder in range(decoders):
        slot = rank_ref[owned_by(list_ref, owner_ref, decoder, my_x)]
        target_ref[slot] = decoder % dp_count * n + (my_x ^ (decoder // dp_count))
    for c in range(chunks):
        loads[c].wait()
        rows = flat_ref[: tiles * LANES, c * span : (c + 1) * span].T
        rope = flat_ref[tiles * LANES :, c * span : (c + 1) * span]
        moved = jnp.concatenate([rope[:, half:], rope[:, :half]], axis=1)
        ropes = jnp.concatenate([rope, moved], axis=0).T
        for i in range(slots):
            slot = c * slots + i
            mine = rows[i * capacity : (i + 1) * capacity, :]
            for t in range(tiles):
                block_ref[slot, t * capacity : (t + 1) * capacity, :] = mine[
                    :, t * LANES : (t + 1) * LANES
                ]
            block_ref[slot, tiles * capacity :, :] = ropes[i * capacity : i * capacity + half, :]
            pltpu.make_async_copy(
                block_ref.at[slot], out_ref.at[target_ref[slot]], out_sem
            ).start()
    pltpu.make_async_copy(block_ref, out_ref, out_sem).wait()


def query_kernel(dp_count, owner_ref, list_ref, len_ref, pos_ref, freq_ref, query_hbm, new_hbm,
                 w_hbm, *refs):
    out_refs, order_ref = refs[:4], refs[4]
    full_ref, rope_ref, turn_ref, query_ref, new_ref, w_ref, sems = refs[5:]
    loads = [
        pltpu.make_async_copy(query_hbm, query_ref, sems.at[0]),
        pltpu.make_async_copy(new_hbm, new_ref, sems.at[1]),
        pltpu.make_async_copy(w_hbm, w_ref, sems.at[2]),
    ]
    for load in loads:
        load.start()
    my_x, my_dp, my_z = here()
    n = len(out_refs)
    steps, seq_dev, heads, qk = query_ref.shape
    nope, latent = w_ref.shape[1], w_ref.shape[2]
    rope = qk - nope
    part = rope // 2
    pairs = steps * seq_dev
    rows = pairs * heads
    shape = (pairs, part)
    pair = lax.broadcasted_iota(jnp.int32, shape, 0)
    pos = pair // seq_dev
    for seq in range(seq_dev):
        pos = pos + jnp.where(pair % seq_dev == seq, pos_ref[seq], 0)
    angles = pos.astype(jnp.float32) * freq_ref[...]
    cosine, sine = jnp.cos(angles), jnp.sin(angles)
    along = jnp.concatenate([cosine, cosine], axis=1)
    across = jnp.concatenate([-sine, sine], axis=1)
    turn_ref[:, :rope] = along
    turn_ref[:, rope:] = across
    loads[0].wait()
    queries = query_ref[...].reshape(rows, qk)
    plain = queries[:, :nope]
    head = lax.broadcasted_iota(jnp.int32, (rows, nope), 0) % heads
    spread = jnp.concatenate(
        [jnp.where(head == h, plain, jnp.zeros_like(plain)) for h in range(heads)], axis=1
    )
    for p in range(pairs):
        value = queries[p * heads : (p + 1) * heads, nope:].astype(jnp.float32)
        other = jnp.concatenate([value[:, part:], value[:, :part]], axis=1)
        turned = value * turn_ref[p : p + 1, :rope] + other * turn_ref[p : p + 1, rope:]
        turned = turned.astype(jnp.bfloat16)
        rope_ref[p * heads : (p + 1) * heads, :] = jnp.concatenate([turned, turned], axis=1)
    loads[1].wait()
    fresh = jnp.concatenate([new_ref[s].astype(jnp.float32) for s in range(steps)], axis=0)
    value = fresh[:, latent:]
    other = jnp.concatenate([value[:, part:], value[:, :part]], axis=1)
    turned = value * along + other * across
    fresh = jnp.concatenate(
        [fresh[:, :latent], turned, jnp.zeros_like(turned)], axis=1
    ).astype(jnp.bfloat16)
    loads[2].wait()
    full_ref[...] = jnp.dot(
        spread, w_ref[...].reshape(heads * nope, latent), preferred_element_type=jnp.float32
    ).astype(jnp.bfloat16)
    row = lax.broadcasted_iota(jnp.int32, (16, pairs), 0)
    source = lax.broadcasted_iota(jnp.int32, (16, pairs), 1)
    lane = lax.broadcasted_iota(jnp.int32, (heads, LANES), 1)
    decoder = my_x * dp_count + my_dp
    block = steps * heads
    tiles = latent // LANES
    packed = block * tiles
    for k in range(n):
        group = my_x ^ my_z ^ k
        seq = jnp.int32(0)
        for m in range(1, seq_dev):
            seq = jnp.where(owner_ref[list_ref[m, decoder]] == group, m, seq)
        at = [
            pl.ds(pl.multiple_of((s * seq_dev + seq) * heads, heads), heads)
            for s in range(steps)
        ]
        for s in range(steps):
            for t in range(tiles):
                first = t * block + s * heads
                out_refs[k][first : first + heads, :] = full_ref[
                    at[s], t * LANES : (t + 1) * LANES
                ]
        for s in range(steps // 2):
            out_refs[k][packed + s * heads : packed + (s + 1) * heads, :] = jnp.where(
                lane < rope, rope_ref[at[s], :], rope_ref[at[s + steps // 2], :]
            )
        if k == 0:
            choose = (source // seq_dev == row) & (source % seq_dev == seq)
            chosen = jnp.dot(
                jnp.where(choose, 1.0, 0.0).astype(jnp.bfloat16),
                fresh,
                preferred_element_type=jnp.float32,
            ).astype(jnp.bfloat16)
            first = packed + block // 2
            length = len_ref[list_ref[seq, decoder]]
            line = lax.broadcasted_iota(jnp.int32, (16, LANES), 0)
            parts = jnp.where(
                line == 8, length // 32, jnp.where(line == 9, length % 32, 0)
            ).astype(jnp.bfloat16)
            for t in range(tiles + 1):
                tile = chosen[:, t * LANES : (t + 1) * LANES]
                if t == tiles:
                    tile = tile + parts
                out_refs[k][first + t * 16 : first + (t + 1) * 16, :] = tile
    total = order_ref.shape[0]
    per = total // n
    row = lax.broadcasted_iota(jnp.int32, (total, 1), 0)
    wanted = jnp.zeros((total, 1), jnp.int32)
    for w in range(n):
        for m in range(seq_dev):
            owner = owner_ref[list_ref[m, w * dp_count + my_dp]]
            first = (lax.rem(my_x - owner + n, n) * n + (my_z ^ owner ^ w)) * steps
            here_row = (row // per == w) & (row % seq_dev == m)
            wanted = jnp.where(here_row, first + row % per // seq_dev, wanted)
    source = lax.broadcasted_iota(jnp.int32, (total, total), 1)
    order_ref[...] = jnp.where(source == wanted, 1.0, 0.0).astype(jnp.bfloat16)


def attend_kernel(scale, steps, kv_ref, *refs):
    n = (len(refs) - 4) // 2
    first_ref, piece_refs, out_refs = refs[0], refs[1 : n + 1], refs[n + 1 : 2 * n + 1]
    plain_ref, rope_refs = refs[-3], refs[-2:]
    stripes, packed_rows, _ = kv_ref.shape
    block, latent = out_refs[0].shape
    tiles = latent // LANES
    half = packed_rows - 2 * tiles * (packed_rows // (2 * tiles + 1))
    capacity = 2 * half
    heads = block // steps
    packed = tiles * block
    lane = lax.broadcasted_iota(jnp.int32, (block // 2, LANES), 1)
    low = lane < LANES // 2
    for k in range(n):
        at = k
        for t in range(tiles):
            plain_ref[at, :, t * LANES : (t + 1) * LANES] = piece_refs[k][
                t * block : (t + 1) * block, :
            ]
        rope = piece_refs[k][packed : packed + block // 2, :]
        swapped = jnp.concatenate([rope[:, LANES // 2 :], rope[:, : LANES // 2]], axis=1)
        blank = jnp.zeros_like(rope)
        rope_refs[0][at, : block // 2, :] = jnp.where(low, rope, blank)
        rope_refs[0][at, block // 2 :, :] = jnp.where(low, swapped, blank)
        rope_refs[1][at, : block // 2, :] = jnp.where(low, blank, swapped)
        rope_refs[1][at, block // 2 :, :] = jnp.where(low, blank, rope)
    plain = plain_ref[...].reshape(n * block, latent)
    sides = [
        jnp.concatenate([plain, ref[...].reshape(n * block, LANES)], axis=1) for ref in rope_refs
    ]
    first = packed + block // 2
    fresh = jnp.concatenate(
        [first_ref[first + t * 16 : first + (t + 1) * 16, :] for t in range(tiles + 1)], axis=1
    )
    parts = fresh[8:10, latent:].astype(jnp.float32).astype(jnp.int32)
    length = parts[:1] * 32 + parts[1:]
    length = jnp.concatenate([length] * (stripes * half // LANES), axis=1)
    rope_keys = kv_ref[:, tiles * capacity :, :].reshape(stripes * half, LANES)
    scores, values = [], []
    for side in range(2):
        parts = [
            kv_ref[:, t * capacity + side * half : t * capacity + (side + 1) * half, :].reshape(
                stripes * half, LANES
            )
            for t in range(tiles)
        ]
        latents = jnp.concatenate(parts, axis=1)
        values.append(latents)
        keys = jnp.concatenate([latents, rope_keys], axis=1)
        score = lax.dot_general(
            sides[side], keys, (((1,), (1,)), ((), ())), preferred_element_type=jnp.float32
        )
        key_id = lax.broadcasted_iota(jnp.int32, (1, stripes * half), 1)
        position = (side * half + key_id % half) * stripes + key_id // half
        scores.append(jnp.where(position < length, score, -jnp.inf))
    score = lax.dot_general(
        sides[0], fresh, (((1,), (1,)), ((), ())), preferred_element_type=jnp.float32
    )
    step = lax.broadcasted_iota(jnp.int32, score.shape, 0) // heads % steps
    new_id = lax.broadcasted_iota(jnp.int32, score.shape, 1)
    scores.append(jnp.where(new_id <= step, score, -jnp.inf))
    values.append(fresh[:, :latent])
    peak = jnp.maximum(
        jnp.max(jnp.maximum(scores[0], scores[1]), axis=1, keepdims=True),
        jnp.max(scores[2], axis=1, keepdims=True),
    )
    turn = scale * math.log2(math.e)
    weights = [jnp.exp2((score - peak) * turn) for score in scores]
    total = jnp.sum(weights[0] + weights[1], axis=1, keepdims=True) + jnp.sum(
        weights[2], axis=1, keepdims=True
    )
    share = 1.0 / total
    mixed = sum(
        jnp.dot((weight * share).astype(jnp.bfloat16), value, preferred_element_type=jnp.float32)
        for weight, value in zip(weights, values)
    ).astype(jnp.bfloat16)
    for j in range(n):
        out_refs[j][...] = mixed[j * block : (j + 1) * block, :]


def values_kernel(w_ref, *refs):
    n = 4
    piece_refs, out_ref = refs[:n], refs[n]
    heads, latent, width = w_ref.shape
    steps = piece_refs[0].shape[0] // heads
    pieces = [
        piece[...].astype(jnp.float32).reshape(steps, heads, latent) for piece in piece_refs
    ]
    stacked = jnp.concatenate(pieces, axis=0)
    by_head = jnp.swapaxes(stacked, 0, 1).astype(jnp.bfloat16)
    for h in range(heads):
        out_ref[:, h * width : (h + 1) * width] = jnp.dot(
            by_head[h], w_ref[h], preferred_element_type=jnp.float32
        ).astype(jnp.bfloat16)


def project_kernel(order_ref, w_ref, *refs):
    n = 4
    piece_refs, out_ref = refs[:n], refs[n]
    per = piece_refs[0].shape[0]
    columns, span = w_ref.shape[1], 256
    gathered = jnp.concatenate([piece[...] for piece in piece_refs], axis=0)
    ordered = jnp.dot(
        order_ref[...], gathered, preferred_element_type=jnp.float32
    ).astype(jnp.bfloat16)
    for first in range(0, columns, span):
        part = jnp.dot(
            ordered, w_ref[:, first : first + span], preferred_element_type=jnp.float32
        ).astype(jnp.bfloat16)
        for w in range(n):
            for z in range(n):
                out_ref[w * n + z, :, first : first + span] = part[w * per : (w + 1) * per, :]


def load_kernel(after_ref, far_ref, near_ref, sem):
    load = pltpu.make_async_copy(far_ref, near_ref, sem)
    load.start()
    load.wait()


def bring_near(weight, after, room, name):
    return pl.pallas_call(
        load_kernel,
        out_shape=jax.ShapeDtypeStruct(weight.shape, weight.dtype),
        in_specs=[VMEM, HBM],
        out_specs=VMEM,
        scratch_shapes=[pltpu.SemaphoreType.DMA],
        compiler_params=pltpu.CompilerParams(vmem_limit_bytes=room * MIB),
        cost_estimate=pl.CostEstimate(
            flops=0, bytes_accessed=4 * weight.size, transcendentals=0
        ),
        name=name,
    )(after, weight)


def final_kernel(piece_ref, out_ref):
    n = 4
    steps, seq_dev, _ = out_ref.shape
    columns = piece_ref.shape[2]
    for x in range(n):
        summed = sum(piece_ref[x * n + h].astype(jnp.float32) for h in range(n))
        summed = summed.astype(jnp.bfloat16)
        for s in range(steps):
            out_ref[s, :, x * columns : (x + 1) * columns] = summed[
                s * seq_dev : (s + 1) * seq_dev, :
            ]


def shards(
    prompt_kv, prompt_len, prefill_owner, decode_list, positions, query, new_kv, w_uk, w_uv, w_out
):
    n = lax.axis_size("pf")
    dp_count = lax.axis_size("dp")
    stripes = dp_count * n
    decoders, seq_dev = decode_list.shape
    requests = decoders * seq_dev
    kv_width = prompt_kv.shape[3]
    total = prompt_kv.shape[2]
    capacity = total // decoders
    step_count, _, head_dev, qk_width = query.shape
    latent = w_uk.shape[2]
    rope_width = kv_width - latent
    served = decode_list.T

    packed_rows = capacity * kv_width // LANES
    outgoing = pl.pallas_call(
        functools.partial(pack_kernel, dp_count, n),
        out_shape=jax.ShapeDtypeStruct((stripes, packed_rows, LANES), prompt_kv.dtype),
        in_specs=[HBM] * 3,
        out_specs=HBM,
        scratch_shapes=[
            pltpu.SMEM((requests,), jnp.int32),
            pltpu.SMEM((seq_dev, decoders), jnp.int32),
            pltpu.SMEM((requests,), jnp.int32),
            pltpu.SMEM((decoders,), jnp.int32),
            pltpu.VMEM((kv_width, total), jnp.bfloat16),
            pltpu.VMEM((stripes, packed_rows, LANES), jnp.bfloat16),
            pltpu.SemaphoreType.DMA((2,)),
            pltpu.SemaphoreType.DMA((2,)),
            pltpu.SemaphoreType.DMA,
        ],
        compiler_params=pltpu.CompilerParams(vmem_limit_bytes=FULL),
        name="pack_rows",
    )(prefill_owner, served, prompt_kv[0, 0].T)
    arrived = lax.all_to_all(outgoing, ("dp", "head"), split_axis=0, concat_axis=0, tiled=True)

    ratio = np.arange(rope_width // 2, dtype=np.float64) * 2.0 / rope_width
    frequency = jnp.asarray((ROPE_BASE**-ratio).astype(np.float32))
    rows = step_count * head_dev
    packed_query = rows * latent // LANES + rows // 2
    extra = 16 * (latent // LANES + 1)
    all_rows = n * seq_dev * step_count
    *pieces, order = pl.pallas_call(
        functools.partial(query_kernel, dp_count),
        out_shape=[
            jax.ShapeDtypeStruct((packed_query + (extra if k == 0 else 0), LANES), jnp.bfloat16)
            for k in range(n)
        ]
        + [jax.ShapeDtypeStruct((all_rows, all_rows), jnp.bfloat16)],
        in_specs=[SMEM, SMEM, SMEM, SMEM, VMEM] + [HBM] * 3,
        out_specs=[VMEM] * (n + 1),
        scratch_shapes=[
            pltpu.VMEM((seq_dev * rows, latent), jnp.bfloat16),
            pltpu.VMEM((seq_dev * rows, LANES), jnp.bfloat16),
            pltpu.VMEM((step_count * seq_dev, 2 * rope_width), jnp.float32),
            pltpu.VMEM(query.shape, query.dtype),
            pltpu.VMEM(new_kv.shape, new_kv.dtype),
            pltpu.VMEM(w_uk.shape, w_uk.dtype),
            pltpu.SemaphoreType.DMA((3,)),
        ],
        compiler_params=pltpu.CompilerParams(vmem_limit_bytes=FULL),
        name="project_queries",
    )(prefill_owner, served, prompt_len, positions, frequency[None, :], query, new_kv, w_uk)
    got = {k: plane(pieces[k], n, lambda x, z, k=k: (x ^ z ^ k, z ^ k)) for k in (0, 2, 1, 3)}

    def attend(picked, name):
        m = len(picked)
        return pl.pallas_call(
            functools.partial(attend_kernel, qk_width ** (-0.5), step_count),
            out_shape=[jax.ShapeDtypeStruct((rows, latent), jnp.bfloat16)] * m,
            in_specs=[VMEM] * (m + 2),
            out_specs=[VMEM] * m,
            scratch_shapes=[
                pltpu.VMEM((m, rows, latent), jnp.bfloat16),
                pltpu.VMEM((m, rows, LANES), jnp.bfloat16),
                pltpu.VMEM((m, rows, LANES), jnp.bfloat16),
            ],
            compiler_params=pltpu.CompilerParams(vmem_limit_bytes=12 * MIB),
            name=name,
        )(arrived, got[0], *[got[k] for k in picked])

    mine, far = attend((0, 2), "attend_first")
    far = swap(far, "head", n, 2)
    near_one, near_two = attend((1, 3), "attend_second")
    w_uv = bring_near(w_uv, near_one, 50, "load_w_uv")

    back = [mine, swap(near_one, "head", n, 1), far, swap(near_two, "head", n, 3)]
    attended = pl.pallas_call(
        values_kernel,
        out_shape=jax.ShapeDtypeStruct(
            (n * step_count, head_dev * w_uv.shape[2]), jnp.bfloat16
        ),
        in_specs=[VMEM] * (n + 1),
        out_specs=VMEM,
        compiler_params=pltpu.CompilerParams(vmem_limit_bytes=12 * MIB),
        name="project_values",
    )(w_uv, *back)
    gathered = [ring(attended, "pf", n, i) for i in range(n)]
    w_out = bring_near(w_out, attended, 43, "load_w_out")
    columns = w_out.shape[1]
    partial_value = pl.pallas_call(
        project_kernel,
        out_shape=jax.ShapeDtypeStruct((n * n, n * step_count, columns), jnp.bfloat16),
        in_specs=[VMEM] * (n + 2),
        out_specs=VMEM,
        compiler_params=pltpu.CompilerParams(vmem_limit_bytes=12 * MIB),
        name="project_out",
    )(order, w_out, *gathered)
    final = lax.all_to_all(
        partial_value, ("pf", "head"), split_axis=0, concat_axis=0, tiled=True
    )
    return pl.pallas_call(
        final_kernel,
        out_shape=jax.ShapeDtypeStruct((step_count, seq_dev, n * columns), jnp.bfloat16),
        in_specs=[VMEM],
        out_specs=VMEM,
        compiler_params=pltpu.CompilerParams(vmem_limit_bytes=8 * MIB),
        name="assemble",
    )(final)


def solution(mesh):
    placed = (
        P("pf", ("dp", "head"), None, None),
        P(),
        P(),
        P(),
        P(("pf", "dp")),
        P(None, ("pf", "dp"), "head", None),
        P(None, ("pf", "dp"), None),
        P("head", None, None),
        P("head", None, None),
        P("head", "pf"),
    )
    return jax.shard_map(
        shards, mesh=mesh, in_specs=placed, out_specs=P(None, ("pf", "dp"), None), check_vma=False
    )
```

```python
import functools
import math

import jax
import jax.numpy as jnp
import numpy as np
from jax import lax
from jax.experimental import pallas as pl
from jax.experimental.pallas import tpu as pltpu
from jax.sharding import PartitionSpec as P

ROPE_BASE = 50000.0


def ring(value, axis, count, shift):
    if shift % count == 0:
        return value
    return lax.ppermute(value, axis, [(i, (i + shift) % count) for i in range(count)])


def plane(value, count, target):
    pairs = []
    for x in range(count):
        for z in range(count):
            to_x, to_z = target(x, z)
            pairs.append((x * count + z, (to_x % count) * count + to_z % count))
    return lax.ppermute(value, ("pf", "head"), pairs)


SMEM = pl.BlockSpec(memory_space=pltpu.SMEM)
VMEM = pl.BlockSpec(memory_space=pltpu.VMEM)
HBM = pl.BlockSpec(memory_space=pltpu.HBM)
LANES = 128
MIB = 1024 * 1024
FULL = 125 * MIB // 2


def here():
    return lax.axis_index("pf"), lax.axis_index("dp"), lax.axis_index("head")


def owned_by(list_ref, owner_ref, decoder, group):
    found = list_ref[0, decoder]
    for n in range(1, list_ref.shape[0]):
        request = list_ref[n, decoder]
        found = jnp.where(owner_ref[request] == group, request, found)
    return found


def pack_kernel(dp_count, n, owner_hbm, list_hbm, prompt_ref, out_ref, owner_ref, list_ref,
                rank_ref, target_ref, flat_ref, block_ref, small_sems, in_sems, out_sem):
    seq_dev, decoders = list_ref.shape
    width, total = flat_ref.shape
    capacity = total // decoders
    tiles = width // LANES
    half = capacity // 2
    chunks = in_sems.shape[0]
    span = total // chunks
    slots = decoders // chunks
    my_x, _, _ = here()
    scalars = [
        pltpu.make_async_copy(owner_hbm, owner_ref, small_sems.at[0]),
        pltpu.make_async_copy(list_hbm, list_ref, small_sems.at[1]),
    ]
    for load in scalars:
        load.start()
    loads = []
    for c in range(chunks):
        at = slice(c * span, (c + 1) * span)
        load = pltpu.make_async_copy(prompt_ref.at[:, at], flat_ref.at[:, at], in_sems.at[c])
        load.start()
        loads.append(load)
    for load in scalars:
        load.wait()
    count = jnp.int32(0)
    for request in range(decoders * seq_dev):
        rank_ref[request] = count
        count = count + jnp.where(owner_ref[request] == my_x, 1, 0)
    for decoder in range(decoders):
        slot = rank_ref[owned_by(list_ref, owner_ref, decoder, my_x)]
        target_ref[slot] = decoder % dp_count * n + decoder // dp_count
    for c in range(chunks):
        loads[c].wait()
        rows = flat_ref[: tiles * LANES, c * span : (c + 1) * span].T
        rope = flat_ref[tiles * LANES :, c * span : (c + 1) * span]
        moved = jnp.concatenate([rope[:, half:], rope[:, :half]], axis=1)
        ropes = jnp.concatenate([rope, moved], axis=0).T
        for i in range(slots):
            slot = c * slots + i
            mine = rows[i * capacity : (i + 1) * capacity, :]
            for t in range(tiles):
                block_ref[slot, t * capacity : (t + 1) * capacity, :] = mine[
                    :, t * LANES : (t + 1) * LANES
                ]
            block_ref[slot, tiles * capacity :, :] = ropes[i * capacity : i * capacity + half, :]
            pltpu.make_async_copy(
                block_ref.at[slot], out_ref.at[target_ref[slot]], out_sem
            ).start()
    pltpu.make_async_copy(block_ref, out_ref, out_sem).wait()


def query_kernel(dp_count, owner_ref, list_ref, len_ref, pos_ref, freq_ref, query_hbm, new_hbm,
                 w_hbm, *refs):
    out_refs, order_ref = refs[:4], refs[4]
    full_ref, rope_ref, turn_ref, query_ref, new_ref, w_ref, sems = refs[5:]
    loads = [
        pltpu.make_async_copy(query_hbm, query_ref, sems.at[0]),
        pltpu.make_async_copy(new_hbm, new_ref, sems.at[1]),
        pltpu.make_async_copy(w_hbm, w_ref, sems.at[2]),
    ]
    for load in loads:
        load.start()
    my_x, my_dp, my_z = here()
    n = len(out_refs)
    steps, seq_dev, heads, qk = query_ref.shape
    nope, latent = w_ref.shape[1], w_ref.shape[2]
    rope = qk - nope
    part = rope // 2
    pairs = steps * seq_dev
    rows = pairs * heads
    shape = (pairs, part)
    pair = lax.broadcasted_iota(jnp.int32, shape, 0)
    pos = pair // seq_dev
    for seq in range(seq_dev):
        pos = pos + jnp.where(pair % seq_dev == seq, pos_ref[seq], 0)
    angles = pos.astype(jnp.float32) * freq_ref[...]
    cosine, sine = jnp.cos(angles), jnp.sin(angles)
    along = jnp.concatenate([cosine, cosine], axis=1)
    across = jnp.concatenate([-sine, sine], axis=1)
    turn_ref[:, :rope] = along
    turn_ref[:, rope:] = across
    loads[0].wait()
    queries = query_ref[...].reshape(rows, qk)
    plain = queries[:, :nope]
    head = lax.broadcasted_iota(jnp.int32, (rows, nope), 0) % heads
    spread = jnp.concatenate(
        [jnp.where(head == h, plain, jnp.zeros_like(plain)) for h in range(heads)], axis=1
    )
    for p in range(pairs):
        value = queries[p * heads : (p + 1) * heads, nope:].astype(jnp.float32)
        other = jnp.concatenate([value[:, part:], value[:, :part]], axis=1)
        turned = value * turn_ref[p : p + 1, :rope] + other * turn_ref[p : p + 1, rope:]
        turned = turned.astype(jnp.bfloat16)
        rope_ref[p * heads : (p + 1) * heads, :] = jnp.concatenate([turned, turned], axis=1)
    loads[1].wait()
    fresh = jnp.concatenate([new_ref[s].astype(jnp.float32) for s in range(steps)], axis=0)
    value = fresh[:, latent:]
    other = jnp.concatenate([value[:, part:], value[:, :part]], axis=1)
    turned = value * along + other * across
    fresh = jnp.concatenate(
        [fresh[:, :latent], turned, jnp.zeros_like(turned)], axis=1
    ).astype(jnp.bfloat16)
    loads[2].wait()
    full_ref[...] = jnp.dot(
        spread, w_ref[...].reshape(heads * nope, latent), preferred_element_type=jnp.float32
    ).astype(jnp.bfloat16)
    row = lax.broadcasted_iota(jnp.int32, (16, pairs), 0)
    source = lax.broadcasted_iota(jnp.int32, (16, pairs), 1)
    lane = lax.broadcasted_iota(jnp.int32, (heads, LANES), 1)
    decoder = my_x * dp_count + my_dp
    block = steps * heads
    tiles = latent // LANES
    packed = block * tiles
    for k in range(n):
        group = lax.rem(my_z + k, n)
        seq = jnp.int32(0)
        for m in range(1, seq_dev):
            seq = jnp.where(owner_ref[list_ref[m, decoder]] == group, m, seq)
        at = [
            pl.ds(pl.multiple_of((s * seq_dev + seq) * heads, heads), heads)
            for s in range(steps)
        ]
        for s in range(steps):
            for t in range(tiles):
                first = t * block + s * heads
                out_refs[k][first : first + heads, :] = full_ref[
                    at[s], t * LANES : (t + 1) * LANES
                ]
        for s in range(steps // 2):
            out_refs[k][packed + s * heads : packed + (s + 1) * heads, :] = jnp.where(
                lane < rope, rope_ref[at[s], :], rope_ref[at[s + steps // 2], :]
            )
        if k == 0:
            choose = (source // seq_dev == row) & (source % seq_dev == seq)
            chosen = jnp.dot(
                jnp.where(choose, 1.0, 0.0).astype(jnp.bfloat16),
                fresh,
                preferred_element_type=jnp.float32,
            ).astype(jnp.bfloat16)
            first = packed + block // 2
            length = len_ref[list_ref[seq, decoder]]
            line = lax.broadcasted_iota(jnp.int32, (16, LANES), 0)
            parts = jnp.where(
                line == 8, length // 32, jnp.where(line == 9, length % 32, 0)
            ).astype(jnp.bfloat16)
            for t in range(tiles + 1):
                tile = chosen[:, t * LANES : (t + 1) * LANES]
                if t == tiles:
                    tile = tile + parts
                out_refs[k][first + t * 16 : first + (t + 1) * 16, :] = tile
    total = order_ref.shape[0]
    per = total // n
    row = lax.broadcasted_iota(jnp.int32, (total, 1), 0)
    wanted = jnp.zeros((total, 1), jnp.int32)
    for w in range(n):
        for m in range(seq_dev):
            owner = owner_ref[list_ref[m, w * dp_count + my_dp]]
            first = (lax.rem(my_x - owner + n, n) * n + lax.rem(my_z - w + n, n)) * steps
            here_row = (row // per == w) & (row % seq_dev == m)
            wanted = jnp.where(here_row, first + row % per // seq_dev, wanted)
    source = lax.broadcasted_iota(jnp.int32, (total, total), 1)
    order_ref[...] = jnp.where(source == wanted, 1.0, 0.0).astype(jnp.bfloat16)


def attend_kernel(scale, steps, kv_ref, *refs):
    n = 4
    piece_refs, out_refs, plain_ref, rope_refs = refs[:n], refs[n : 2 * n], refs[2 * n], refs[-2:]
    my_x, _, my_z = here()
    stripes, packed_rows, _ = kv_ref.shape
    block, latent = out_refs[0].shape
    tiles = latent // LANES
    half = packed_rows - 2 * tiles * (packed_rows // (2 * tiles + 1))
    capacity = 2 * half
    heads = block // steps
    packed = tiles * block
    lane = lax.broadcasted_iota(jnp.int32, (block // 2, LANES), 1)
    low = lane < LANES // 2
    for k in range(n):
        at = lax.rem(my_x - my_z - k + 2 * n, n)
        for t in range(tiles):
            plain_ref[at, :, t * LANES : (t + 1) * LANES] = piece_refs[k][
                t * block : (t + 1) * block, :
            ]
        rope = piece_refs[k][packed : packed + block // 2, :]
        swapped = jnp.concatenate([rope[:, LANES // 2 :], rope[:, : LANES // 2]], axis=1)
        blank = jnp.zeros_like(rope)
        rope_refs[0][at, : block // 2, :] = jnp.where(low, rope, blank)
        rope_refs[0][at, block // 2 :, :] = jnp.where(low, swapped, blank)
        rope_refs[1][at, : block // 2, :] = jnp.where(low, blank, swapped)
        rope_refs[1][at, block // 2 :, :] = jnp.where(low, blank, rope)
    plain = plain_ref[...].reshape(n * block, latent)
    sides = [
        jnp.concatenate([plain, ref[...].reshape(n * block, LANES)], axis=1) for ref in rope_refs
    ]
    first = packed + block // 2
    fresh = jnp.concatenate(
        [piece_refs[0][first + t * 16 : first + (t + 1) * 16, :] for t in range(tiles + 1)], axis=1
    )
    parts = fresh[8:10, latent:].astype(jnp.float32).astype(jnp.int32)
    length = parts[:1] * 32 + parts[1:]
    length = jnp.concatenate([length] * (stripes * half // LANES), axis=1)
    rope_keys = kv_ref[:, tiles * capacity :, :].reshape(stripes * half, LANES)
    scores, values = [], []
    for side in range(2):
        parts = [
            kv_ref[:, t * capacity + side * half : t * capacity + (side + 1) * half, :].reshape(
                stripes * half, LANES
            )
            for t in range(tiles)
        ]
        latents = jnp.concatenate(parts, axis=1)
        values.append(latents)
        keys = jnp.concatenate([latents, rope_keys], axis=1)
        score = lax.dot_general(
            sides[side], keys, (((1,), (1,)), ((), ())), preferred_element_type=jnp.float32
        )
        key_id = lax.broadcasted_iota(jnp.int32, (1, stripes * half), 1)
        position = (side * half + key_id % half) * stripes + key_id // half
        scores.append(jnp.where(position < length, score, -jnp.inf))
    score = lax.dot_general(
        sides[0], fresh, (((1,), (1,)), ((), ())), preferred_element_type=jnp.float32
    )
    step = lax.broadcasted_iota(jnp.int32, score.shape, 0) // heads % steps
    new_id = lax.broadcasted_iota(jnp.int32, score.shape, 1)
    scores.append(jnp.where(new_id <= step, score, -jnp.inf))
    values.append(fresh[:, :latent])
    peak = jnp.maximum(
        jnp.max(jnp.maximum(scores[0], scores[1]), axis=1, keepdims=True),
        jnp.max(scores[2], axis=1, keepdims=True),
    )
    turn = scale * math.log2(math.e)
    weights = [jnp.exp2((score - peak) * turn) for score in scores]
    total = jnp.sum(weights[0] + weights[1], axis=1, keepdims=True) + jnp.sum(
        weights[2], axis=1, keepdims=True
    )
    share = 1.0 / total
    mixed = sum(
        jnp.dot((weight * share).astype(jnp.bfloat16), value, preferred_element_type=jnp.float32)
        for weight, value in zip(weights, values)
    ).astype(jnp.bfloat16)
    for j in range(n):
        out_refs[j][...] = mixed[j * block : (j + 1) * block, :]


def values_kernel(w_ref, *refs):
    n = 4
    piece_refs, out_ref = refs[:n], refs[n]
    heads, latent, width = w_ref.shape
    steps = piece_refs[0].shape[0] // heads
    pieces = [
        piece[...].astype(jnp.float32).reshape(steps, heads, latent) for piece in piece_refs
    ]
    stacked = jnp.concatenate(pieces, axis=0)
    by_head = jnp.swapaxes(stacked, 0, 1).astype(jnp.bfloat16)
    for h in range(heads):
        out_ref[:, h * width : (h + 1) * width] = jnp.dot(
            by_head[h], w_ref[h], preferred_element_type=jnp.float32
        ).astype(jnp.bfloat16)


def project_kernel(order_ref, w_ref, *refs):
    n = 4
    piece_refs, out_ref = refs[:n], refs[n]
    per = piece_refs[0].shape[0]
    columns, span = w_ref.shape[1], 256
    gathered = jnp.concatenate([piece[...] for piece in piece_refs], axis=0)
    ordered = jnp.dot(
        order_ref[...], gathered, preferred_element_type=jnp.float32
    ).astype(jnp.bfloat16)
    for first in range(0, columns, span):
        part = jnp.dot(
            ordered, w_ref[:, first : first + span], preferred_element_type=jnp.float32
        ).astype(jnp.bfloat16)
        for w in range(n):
            for z in range(n):
                out_ref[w * n + z, :, first : first + span] = part[w * per : (w + 1) * per, :]


def load_kernel(after_ref, far_ref, near_ref, sem):
    load = pltpu.make_async_copy(far_ref, near_ref, sem)
    load.start()
    load.wait()


def bring_near(weight, after, room, name):
    return pl.pallas_call(
        load_kernel,
        out_shape=jax.ShapeDtypeStruct(weight.shape, weight.dtype),
        in_specs=[VMEM, HBM],
        out_specs=VMEM,
        scratch_shapes=[pltpu.SemaphoreType.DMA],
        compiler_params=pltpu.CompilerParams(vmem_limit_bytes=room * MIB),
        cost_estimate=pl.CostEstimate(
            flops=0, bytes_accessed=4 * weight.size, transcendentals=0
        ),
        name=name,
    )(after, weight)


def final_kernel(piece_ref, out_ref):
    n = 4
    steps, seq_dev, _ = out_ref.shape
    columns = piece_ref.shape[2]
    for x in range(n):
        summed = sum(piece_ref[x * n + h].astype(jnp.float32) for h in range(n))
        summed = summed.astype(jnp.bfloat16)
        for s in range(steps):
            out_ref[s, :, x * columns : (x + 1) * columns] = summed[
                s * seq_dev : (s + 1) * seq_dev, :
            ]


def shards(
    prompt_kv, prompt_len, prefill_owner, decode_list, positions, query, new_kv, w_uk, w_uv, w_out
):
    n = lax.axis_size("pf")
    dp_count = lax.axis_size("dp")
    stripes = dp_count * n
    decoders, seq_dev = decode_list.shape
    requests = decoders * seq_dev
    kv_width = prompt_kv.shape[3]
    total = prompt_kv.shape[2]
    capacity = total // decoders
    step_count, _, head_dev, qk_width = query.shape
    latent = w_uk.shape[2]
    rope_width = kv_width - latent
    served = decode_list.T

    packed_rows = capacity * kv_width // LANES
    outgoing = pl.pallas_call(
        functools.partial(pack_kernel, dp_count, n),
        out_shape=jax.ShapeDtypeStruct((stripes, packed_rows, LANES), prompt_kv.dtype),
        in_specs=[HBM] * 3,
        out_specs=HBM,
        scratch_shapes=[
            pltpu.SMEM((requests,), jnp.int32),
            pltpu.SMEM((seq_dev, decoders), jnp.int32),
            pltpu.SMEM((requests,), jnp.int32),
            pltpu.SMEM((decoders,), jnp.int32),
            pltpu.VMEM((kv_width, total), jnp.bfloat16),
            pltpu.VMEM((stripes, packed_rows, LANES), jnp.bfloat16),
            pltpu.SemaphoreType.DMA((2,)),
            pltpu.SemaphoreType.DMA((4,)),
            pltpu.SemaphoreType.DMA,
        ],
        compiler_params=pltpu.CompilerParams(vmem_limit_bytes=FULL),
        name="pack_rows",
    )(prefill_owner, served, prompt_kv[0, 0].T)
    arrived = lax.all_to_all(outgoing, ("dp", "head"), split_axis=0, concat_axis=0, tiled=True)

    ratio = np.arange(rope_width // 2, dtype=np.float64) * 2.0 / rope_width
    frequency = jnp.asarray((ROPE_BASE**-ratio).astype(np.float32))
    rows = step_count * head_dev
    packed_query = rows * latent // LANES + rows // 2
    extra = 16 * (latent // LANES + 1)
    all_rows = n * seq_dev * step_count
    *pieces, order = pl.pallas_call(
        functools.partial(query_kernel, dp_count),
        out_shape=[
            jax.ShapeDtypeStruct((packed_query + (extra if k == 0 else 0), LANES), jnp.bfloat16)
            for k in range(n)
        ]
        + [jax.ShapeDtypeStruct((all_rows, all_rows), jnp.bfloat16)],
        in_specs=[SMEM, SMEM, SMEM, SMEM, VMEM] + [HBM] * 3,
        out_specs=[VMEM] * (n + 1),
        scratch_shapes=[
            pltpu.VMEM((seq_dev * rows, latent), jnp.bfloat16),
            pltpu.VMEM((seq_dev * rows, LANES), jnp.bfloat16),
            pltpu.VMEM((step_count * seq_dev, 2 * rope_width), jnp.float32),
            pltpu.VMEM(query.shape, query.dtype),
            pltpu.VMEM(new_kv.shape, new_kv.dtype),
            pltpu.VMEM(w_uk.shape, w_uk.dtype),
            pltpu.SemaphoreType.DMA((3,)),
        ],
        compiler_params=pltpu.CompilerParams(vmem_limit_bytes=FULL),
        name="project_queries",
    )(prefill_owner, served, prompt_len, positions, frequency[None, :], query, new_kv, w_uk)
    got = {k: plane(pieces[k], n, lambda x, z, k=k: (z + k, x)) for k in (2, 1, 3, 0)}
    got = [got[k] for k in range(n)]

    latent_out = pl.pallas_call(
        functools.partial(attend_kernel, qk_width ** (-0.5), step_count),
        out_shape=[jax.ShapeDtypeStruct((rows, latent), jnp.bfloat16)] * n,
        in_specs=[VMEM] * (n + 1),
        out_specs=[VMEM] * n,
        scratch_shapes=[
            pltpu.VMEM((n, rows, latent), jnp.bfloat16),
            pltpu.VMEM((n, rows, LANES), jnp.bfloat16),
            pltpu.VMEM((n, rows, LANES), jnp.bfloat16),
        ],
        compiler_params=pltpu.CompilerParams(vmem_limit_bytes=12 * MIB),
        name="attend",
    )(arrived, *got)
    w_uv = bring_near(w_uv, latent_out[0], 50, "load_w_uv")

    back = [ring(latent_out[j], "head", n, j) for j in range(n)]
    attended = pl.pallas_call(
        values_kernel,
        out_shape=jax.ShapeDtypeStruct(
            (n * step_count, head_dev * w_uv.shape[2]), jnp.bfloat16
        ),
        in_specs=[VMEM] * (n + 1),
        out_specs=VMEM,
        compiler_params=pltpu.CompilerParams(vmem_limit_bytes=12 * MIB),
        name="project_values",
    )(w_uv, *back)
    gathered = [ring(attended, "pf", n, i) for i in range(n)]
    w_out = bring_near(w_out, attended, 43, "load_w_out")
    columns = w_out.shape[1]
    partial_value = pl.pallas_call(
        project_kernel,
        out_shape=jax.ShapeDtypeStruct((n * n, n * step_count, columns), jnp.bfloat16),
        in_specs=[VMEM] * (n + 2),
        out_specs=VMEM,
        compiler_params=pltpu.CompilerParams(vmem_limit_bytes=12 * MIB),
        name="project_out",
    )(order, w_out, *gathered)
    final = lax.all_to_all(
        partial_value, ("pf", "head"), split_axis=0, concat_axis=0, tiled=True
    )
    return pl.pallas_call(
        final_kernel,
        out_shape=jax.ShapeDtypeStruct((step_count, seq_dev, n * columns), jnp.bfloat16),
        in_specs=[VMEM],
        out_specs=VMEM,
        compiler_params=pltpu.CompilerParams(vmem_limit_bytes=8 * MIB),
        name="assemble",
    )(final)


def solution(mesh):
    placed = (
        P("pf", ("dp", "head"), None, None),
        P(),
        P(),
        P(),
        P(("pf", "dp")),
        P(None, ("pf", "dp"), "head", None),
        P(None, ("pf", "dp"), None),
        P("head", None, None),
        P("head", None, None),
        P("head", "pf"),
    )
    return jax.shard_map(
        shards, mesh=mesh, in_specs=placed, out_specs=P(None, ("pf", "dp"), None), check_vma=False
    )
```
